32 devices in a mesh: group: 4 (over z), tensor: 8 (over y, x, core).
Axes of the slice: x: 2, y: 2, z: 4, core: 2. Of those that a mesh axis runs over, the one named last changes fastest.
Arguments:
- hidden: bfloat16 [6144, 2048], P(('group', 'tensor')), may hold values from -20 to 20
- request_of: int32 [6144], P('group'), may hold values from 0 to 95, as said below
- positions: int32 [6144], P('group'), may hold values from 0 to 511, as said below
- page_table: int32 [4, 64], P('group'), may hold values from 0 to 63, each once within a row
- attn_gain: float32 [2048], replicated, may hold values from 0.5 to 1.5
- mlp_gain: float32 [2048], replicated, may hold values from 0.5 to 1.5
- wq: float32 [2048, 2048], P('group', 'tensor'), may hold values from -2 to 2
- wk: float32 [2048, 1024], P('group', 'tensor'), may hold values from -1 to 1
- wv: float32 [2048, 1024], P('group', 'tensor'), may hold values from -0.125 to 0.125
- wo: float32 [2048, 2048], P('tensor', 'group'), may hold values from -0.125 to 0.125
- w_gate: float32 [2048, 8192], P('group', 'tensor'), may hold values from -0.125 to 0.125
- w_up: float32 [2048, 8192], P('group', 'tensor'), may hold values from -0.125 to 0.125
- w_down: float32 [8192, 2048], P('tensor', 'group'), may hold values from -0.0625 to 0.0625
Outputs:
- layer_out: bfloat16 [6144, 2048], P(('group', 'tensor'))
- kv_pages: bfloat16 [256, 128, 2048], P('group', None, 'tensor')
The draws below stay inside these ranges and needn't reach their ends.
Inputs may be any that keep to these rules, and one draw needn't show every extreme that they name: `request_of`: prompt numbers rise strictly along the token stream, starting at 0, and the last prompt of the stream has the number 6144 // 64 - 1; a prompt's rows are consecutive, and a prompt that reaches the last row of one block of 1536 rows continues at the first row of the next block. A prompt's rows have positions 0, 1, 2 and so on in order; a prompt has at most 512 rows, and one has exactly 512.
All inputs are finite; a program needn't handle non-finite values.
Results may differ from the reference program's by a relative error of at most 0.014.
Values may be sent and summed in bfloat16 or wider, within the bound.
No kernel may reach another device: no remote copies, remote signals or barrier semaphores. Data moves between devices by JAX's collectives and lax.ppermute only.
A program may use at most 128 MiB of HBM per device.

```python
import jax
import jax.numpy as jnp
from jax import lax

D = 2048
QH = 16
KVH = 8
HD = 128
FF = 8192
TOK_GRP = 1536
MAXLEN = 512
MINLEN = 64
PAGE = 128
TOKENS = 6144
PAGES_GRP = 64
N_GROUP = 4


def request_stream(key):
    count = TOKENS // MINLEN + 1
    stream_key = jax.random.fold_in(key, 7101)
    first_key, second_key, third_key = jax.random.split(stream_key, 3)
    expo = jax.random.randint(first_key, (count,), 0, 4)
    extra = jax.random.randint(second_key, (count,), 0, MINLEN)
    lengths = jnp.minimum(MAXLEN, jnp.left_shift(jnp.int32(MINLEN), expo) + extra).astype(jnp.int32)
    longest = jax.random.randint(third_key, (), 0, TOKENS // MAXLEN)
    lengths = lengths.at[longest].set(MAXLEN)
    ends = jnp.cumsum(lengths).astype(jnp.int32)
    rows = jnp.arange(TOKENS, dtype=jnp.int32)
    finished = (ends[None, :] <= rows[:, None]).astype(jnp.int32)
    number = jnp.sum(finished, axis=1).astype(jnp.int32)
    begin = jnp.sum(finished * lengths[None, :], axis=1).astype(jnp.int32)
    final_number = number[TOKENS - 1]
    renamed = jnp.where(number == final_number, jnp.int32(TOKENS // MINLEN - 1), number).astype(jnp.int32)
    return (renamed, (rows - begin).astype(jnp.int32))


def draw_request_of(key, part):
    return request_stream(key)[0]


def draw_positions(key, part):
    return request_stream(key)[1]


def draw_hidden(key, part):
    base_key = jax.random.fold_in(jax.random.fold_in(key, 3301), 0)
    values = jax.random.normal(base_key, (TOKENS, D), jnp.float32)
    return jnp.clip(values, -20.0, 20.0).astype(jnp.bfloat16)


def key_basis(key):
    basis_key = jax.random.fold_in(key, 5501)
    basis = jnp.clip(jax.random.normal(basis_key, (D, KVH, HD), jnp.float32), -6.0, 6.0)
    return basis * D ** (-0.5)


def draw_wk(key, part):
    return jnp.clip(key_basis(key), -1.0, 1.0).reshape(D, KVH * HD)


def draw_wq(key, part):
    own_key = jax.random.fold_in(key, 5502)
    values = jnp.clip(jax.random.normal(own_key, (D, QH, HD), jnp.float32), -6.0, 6.0) * D ** (-0.5)
    return jnp.clip(values, -2.0, 2.0).reshape(D, QH * HD)


def block_levels(rng, shape, shards, least, top_value):
    factor_of, own = 1.0, jax.random.fold_in(rng, 6)
    for axis_at, blocks in shards:
        draws = jnp.exp(jax.random.uniform(jax.random.fold_in(own, axis_at), (blocks,), jnp.float32, least / len(shards), top_value / len(shards)))
        factor_of = factor_of * jnp.repeat(draws, shape[axis_at] // blocks).reshape([-1 if axis == axis_at else 1 for axis in range(len(shape))])
    return factor_of


def gaussian(key, dims, deviation, most, cuts=(), held_as=jnp.bfloat16):
    drawn = deviation * jax.random.normal(key, dims, jnp.float32)
    if cuts:
        drawn = drawn * block_levels(key, dims, cuts, -0.22, 0.18)
    return jnp.clip(drawn, -most, most).astype(held_as)


def setup_inputs(seed: int = 0) -> dict:
    seeds = jax.random.split(jax.random.key(seed), 14)
    return {
        "hidden": draw_hidden(jax.random.fold_in(seeds[13], 71), 0),
        "request_of": draw_request_of(jax.random.fold_in(seeds[13], 71), 0),
        "positions": draw_positions(jax.random.fold_in(seeds[13], 71), 0),
        "page_table": jax.vmap(lambda own: jax.random.permutation(own, PAGES_GRP))(jax.random.split(seeds[3], N_GROUP)).reshape((N_GROUP, PAGES_GRP)).astype(jnp.int32),
        "attn_gain": jnp.clip(jax.random.uniform(seeds[4], (D,), jnp.float32, 0.5, 1.5), 0.5, 1.5),
        "mlp_gain": jnp.clip(jax.random.uniform(seeds[5], (D,), jnp.float32, 0.5, 1.5), 0.5, 1.5),
        "wq": draw_wq(jax.random.fold_in(seeds[13], 71), 0),
        "wk": draw_wk(jax.random.fold_in(seeds[13], 71), 0),
        "wv": gaussian(seeds[8], (D, KVH * HD), D ** -0.5, 0.125, ((0, 4), (1, 8)), jnp.float32),
        "wo": gaussian(seeds[9], (QH * HD, D), (QH * HD) ** -0.5, 0.125, ((0, 8), (1, 4)), jnp.float32),
        "w_gate": gaussian(seeds[10], (D, FF), D ** -0.5, 0.125, ((0, 4), (1, 8)), jnp.float32),
        "w_up": gaussian(seeds[11], (D, FF), D ** -0.5, 0.125, ((0, 4), (1, 8)), jnp.float32),
        "w_down": gaussian(seeds[12], (FF, D), FF ** -0.5, 0.0625, ((0, 8), (1, 4)), jnp.float32),
    }


rope_base = 1000000.0
norm_eps = 1e-06

def rms_scale(values, gain):
    square = lax.optimization_barrier(jnp.mean(values * values, axis=-1, keepdims=True))
    return (values * lax.rsqrt(square + norm_eps) * gain).astype(jnp.bfloat16)

def rotate(values, places):
    half_dim = values.shape[-1] // 2
    frequency = rope_base ** (-(jnp.arange(half_dim, dtype=jnp.float32) * 2.0 / values.shape[-1]))
    angle = places.astype(jnp.float32)[:, None] * frequency[None, :]
    cosine = jnp.cos(angle)[:, None, :]
    sine = jnp.sin(angle)[:, None, :]
    widened = values.astype(jnp.float32)
    first = widened[..., :half_dim]
    second = widened[..., half_dim:]
    return jnp.concatenate([first * cosine - second * sine, second * cosine + first * sine], axis=-1).astype(jnp.bfloat16)

def attend_group(index, queries, keys, values, request_of, positions):
    start = (index * TOK_GRP).astype(jnp.int32)
    before = jnp.maximum(start - TOK_GRP, 0).astype(jnp.int32)
    query_block = lax.dynamic_slice_in_dim(queries, start, TOK_GRP, 0)
    key_block = jnp.concatenate([lax.dynamic_slice_in_dim(keys, before, TOK_GRP, 0), lax.dynamic_slice_in_dim(keys, start, TOK_GRP, 0)], axis=0)
    value_block = jnp.concatenate([lax.dynamic_slice_in_dim(values, before, TOK_GRP, 0), lax.dynamic_slice_in_dim(values, start, TOK_GRP, 0)], axis=0)
    own_request = lax.dynamic_slice_in_dim(request_of, start, TOK_GRP, 0)
    earlier_request = jnp.where(index > 0, lax.dynamic_slice_in_dim(request_of, before, TOK_GRP, 0), -1).astype(jnp.int32)
    key_request = jnp.concatenate([earlier_request, own_request], axis=0)
    own_position = lax.dynamic_slice_in_dim(positions, start, TOK_GRP, 0)
    key_position = jnp.concatenate([lax.dynamic_slice_in_dim(positions, before, TOK_GRP, 0), own_position], axis=0)
    visible = (own_request[:, None] == key_request[None, :]) & (key_position[None, :] <= own_position[:, None])
    ratio = QH // KVH
    key_wide = jnp.repeat(key_block, ratio, axis=1).astype(jnp.float32)
    value_wide = jnp.repeat(value_block, ratio, axis=1).astype(jnp.float32)
    scores = jnp.einsum('qhd,khd->hqk', query_block.astype(jnp.float32), key_wide, precision=lax.Precision.HIGHEST) * HD ** (-0.5)
    scores = jnp.where(visible[None], scores, -1e+30)
    row_peak = lax.optimization_barrier(jnp.max(scores, axis=-1, keepdims=True))
    probs = jnp.where(visible[None], jnp.exp(scores - row_peak), 0.0)
    total = lax.optimization_barrier(jnp.sum(probs, axis=-1, keepdims=True))
    rounded = lax.optimization_barrier(probs.astype(jnp.bfloat16)).astype(jnp.float32)
    mixed_heads = jnp.einsum('hqk,khd->qhd', rounded, value_wide, precision=lax.Precision.HIGHEST) / jnp.transpose(total, (1, 0, 2))
    return mixed_heads.astype(jnp.bfloat16).reshape(TOK_GRP, QH * HD)

def reference(hidden, request_of, positions, page_table, attn_gain, mlp_gain, wq, wk, wv, wo, w_gate, w_up, w_down):
    query_w = wq.astype(jnp.bfloat16)
    key_w = wk.astype(jnp.bfloat16)
    value_w = wv.astype(jnp.bfloat16)
    out_w = wo.astype(jnp.bfloat16)
    gate_w = w_gate.astype(jnp.bfloat16)
    up_w = w_up.astype(jnp.bfloat16)
    down_w = w_down.astype(jnp.bfloat16)
    residual = hidden.astype(jnp.float32)
    normed = rms_scale(residual, attn_gain)
    query_raw = jnp.dot(normed, query_w, preferred_element_type=jnp.float32).astype(jnp.bfloat16).reshape(TOKENS, QH, HD)
    key_raw = jnp.dot(normed, key_w, preferred_element_type=jnp.float32).astype(jnp.bfloat16).reshape(TOKENS, KVH, HD)
    value_rows = jnp.dot(normed, value_w, preferred_element_type=jnp.float32).astype(jnp.bfloat16).reshape(TOKENS, KVH, HD)
    queries = rotate(query_raw, positions)
    keys = rotate(key_raw, positions)

    def one_group(index):
        return attend_group(index, queries, keys, value_rows, request_of, positions)
    attended = lax.map(one_group, jnp.arange(N_GROUP, dtype=jnp.int32)).reshape(TOKENS, QH * HD)
    mixed = residual + jnp.dot(attended, out_w, preferred_element_type=jnp.float32)
    normed_mlp = rms_scale(mixed, mlp_gain)
    gate = jnp.dot(normed_mlp, gate_w, preferred_element_type=jnp.float32)
    upward = jnp.dot(normed_mlp, up_w, preferred_element_type=jnp.float32)
    activation = (jax.nn.silu(gate) * upward).astype(jnp.bfloat16)
    layer_out = (mixed + jnp.dot(activation, down_w, preferred_element_type=jnp.float32)).astype(jnp.bfloat16)
    rows = jnp.arange(TOKENS, dtype=jnp.int32)
    changed = jnp.concatenate([jnp.ones((1,), dtype=bool), request_of[1:] != request_of[:-1]])
    opens = changed | (rows % TOK_GRP == 0) | (positions % PAGE == 0)
    logical = (jnp.cumsum(opens.reshape(N_GROUP, TOK_GRP).astype(jnp.int32), axis=1) - 1).astype(jnp.int32)
    chosen = jnp.take_along_axis(page_table, logical, axis=1).astype(jnp.int32)
    owner = (rows // TOK_GRP).reshape(N_GROUP, TOK_GRP).astype(jnp.int32)
    slots = (positions % PAGE).reshape(N_GROUP, TOK_GRP).astype(jnp.int32)
    target = ((owner * PAGES_GRP + chosen) * PAGE + slots).reshape(TOKENS).astype(jnp.int32)
    kv_rows = jnp.stack([keys, value_rows], axis=2).reshape(TOKENS, KVH * 2 * HD)
    cache = jnp.zeros((N_GROUP * PAGES_GRP * PAGE, KVH * 2 * HD), jnp.bfloat16).at[target].set(kv_rows)
    return (layer_out, cache.reshape(N_GROUP * PAGES_GRP, PAGE, KVH * 2 * HD))
```

```python
import functools

import jax
import jax.numpy as jnp
from jax import lax
from jax.experimental import pallas as pl
from jax.experimental.pallas import tpu as pltpu
from jax.sharding import PartitionSpec as P

QH = 16
KVH = 8
HD = 128
PAGE = 128
REACH = 512

rope_base = 1000000.0
norm_eps = 1e-06

F32 = jnp.float32
BF16 = jnp.bfloat16

ORDER = (0, 2, 4, 6, 1, 3, 5, 7)


def swap(value, distance):
    return lax.ppermute(
        value, "tensor", [(i, i ^ distance) for i in range(lax.axis_size("tensor"))]
    )


def turn(value, distance):
    count = lax.axis_size("group")
    return lax.ppermute(value, "group", [(i, (i + distance) % count) for i in range(count)])


def pair_swap(value):
    return lax.ppermute(value, "group", [(i, i ^ 1) for i in range(lax.axis_size("group"))])


def from_behind(block):
    count = lax.axis_size("group")
    return lax.ppermute(block, "group", [(i, i + 1) for i in range(count - 1)])


def after(value, *others):
    return lax.optimization_barrier((value, *others))[0]


def rms_scale(values, gain):
    square = jnp.mean(values * values, axis=-1, keepdims=True)
    return (values * lax.rsqrt(square + norm_eps) * gain).astype(BF16)


def gather_rows(own):
    half = own.shape[0] // 2
    by_x = swap(own, 2)
    by_y = swap(own, 4)
    far_low = swap(by_x[:half], 4)
    far_high = swap(by_y[half:], 2)
    far = jnp.concatenate([far_low, far_high], axis=0)
    near = jnp.concatenate([own, by_x, by_y], axis=0)
    return jnp.concatenate([near, far, swap(near, 1), swap(far, 1)], axis=0)


def add(first, second):
    return (first.astype(F32) + second.astype(F32)).astype(BF16)


def scatter_sum(mine, other):
    got = swap(other, 1)
    total = add(mine, got)
    rows = total.shape[0] // 4
    width = total.shape[1] // 2
    blocks = total.reshape(4, rows, 2 * width)
    left, right = blocks[:, :, :width], blocks[:, :, width:]
    left_in = swap(jnp.stack([left[1], left[3]]), 2)
    right_in = swap(jnp.stack([right[2], right[3]]), 4)
    left_keep = add(left[0], left_in[0])
    left_on = add(left[2], left_in[1])
    right_keep = add(right[0], right_in[0])
    right_on = add(right[1], right_in[1])
    left_last = swap(left_on, 4)
    right_last = swap(right_on, 2)
    return jnp.concatenate(
        [
            left_keep.astype(F32) + left_last.astype(F32),
            right_keep.astype(F32) + right_last.astype(F32),
        ],
        axis=1,
    )


def project_kernel(place, x_ref, w_ref, cos_ref, sin_ref, q_ref, kv_ref):
    raw = jnp.dot(x_ref[...], w_ref[...], preferred_element_type=F32).astype(BF16)
    cosine = cos_ref[...]
    sine = sin_ref[...]

    def rotated(head):
        wide = raw[:, head * HD : (head + 1) * HD].astype(F32)
        turned = jnp.concatenate([wide[:, HD // 2 :], wide[:, : HD // 2]], axis=1)
        return (wide * cosine + turned * sine).astype(BF16)

    heads = q_ref.shape[1] // HD
    for head in range(heads):
        q_ref[:, head * HD : (head + 1) * HD] = rotated(head)
    kv_ref[:, :HD] = rotated(heads)
    kv_ref[:, HD:] = raw[:, (heads + 1) * HD :]


def project(rows, weight, cosine, sine, places):
    blocks = len(ORDER)
    size = rows.shape[0] // blocks
    depth = rows.shape[1]
    width = weight.shape[1]
    query_width = width - 2 * HD
    there = lambda i, place: (place[i], 0)
    return pl.pallas_call(
        project_kernel,
        grid_spec=pltpu.PrefetchScalarGridSpec(
            num_scalar_prefetch=1,
            grid=(blocks,),
            in_specs=[
                pl.BlockSpec((size, depth), lambda i, place: (i, 0)),
                pl.BlockSpec((depth, width), lambda i, place: (0, 0)),
                pl.BlockSpec((size, HD), there),
                pl.BlockSpec((size, HD), there),
            ],
            out_specs=[
                pl.BlockSpec((size, query_width), there),
                pl.BlockSpec((size, 2 * HD), there),
            ],
        ),
        out_shape=[
            jax.ShapeDtypeStruct((rows.shape[0], query_width), BF16),
            jax.ShapeDtypeStruct((rows.shape[0], 2 * HD), BF16),
        ],
        compiler_params=pltpu.CompilerParams(vmem_limit_bytes=32 * 1024 * 1024),
        cost_estimate=pl.CostEstimate(
            flops=2 * rows.shape[0] * depth * width,
            bytes_accessed=2 * (rows.size + weight.size),
            transcendentals=0,
        ),
        name="project",
    )(places, rows, weight, cosine, sine)


def attend_kernel(q_ref, kv_ref, pos_ref, out_ref):
    step = pl.program_id(0)
    size = q_ref.shape[0]
    span = size + REACH
    window = pl.ds(pl.multiple_of(step * size, size), span)
    keys = kv_ref[window, :HD]
    values = kv_ref[window, HD:]
    row = lax.broadcasted_iota(jnp.int32, (size, span), 0)
    column = lax.broadcasted_iota(jnp.int32, (size, span), 1)
    back = row + REACH - column
    visible = (back >= 0) & (back <= pos_ref[...])
    for head in range(q_ref.shape[1] // HD):
        query = q_ref[:, head * HD : (head + 1) * HD]
        scores = lax.dot_general(
            query, keys, (((1,), (1,)), ((), ())), preferred_element_type=F32
        ) * HD ** (-0.5)
        scores = jnp.where(visible, scores, -1e30)
        peak = jnp.max(scores, axis=1, keepdims=True)
        probs = jnp.exp(scores - peak)
        total = jnp.sum(probs, axis=1, keepdims=True)
        mixed = jnp.dot(probs.astype(BF16), values, preferred_element_type=F32)
        out_ref[:, head * HD : (head + 1) * HD] = (mixed / total).astype(BF16)


def attend(queries, all_kv, positions):
    size = 256
    rows, width = queries.shape
    return pl.pallas_call(
        attend_kernel,
        grid=(rows // size,),
        in_specs=[
            pl.BlockSpec((size, width), lambda i: (i, 0)),
            pl.BlockSpec(all_kv.shape, lambda i: (0, 0)),
            pl.BlockSpec((size, 1), lambda i: (i, 0)),
        ],
        out_specs=pl.BlockSpec((size, width), lambda i: (i, 0)),
        out_shape=jax.ShapeDtypeStruct((rows, width), BF16),
        compiler_params=pltpu.CompilerParams(vmem_limit_bytes=32 * 1024 * 1024),
        cost_estimate=pl.CostEstimate(
            flops=4 * rows * (size + REACH) * width,
            bytes_accessed=4 * rows * width,
            transcendentals=rows * (size + REACH) * width // HD,
        ),
        name="attend",
    )(queries, all_kv, positions[:, None])


def mix_kernel(place, x_ref, w_ref, out_ref):
    out_ref[...] = jnp.dot(x_ref[...], w_ref[...], preferred_element_type=F32).astype(BF16)


def mix(attended, weight, places):
    blocks = places.shape[0]
    size = attended.shape[0] // len(ORDER)
    depth, width = weight.shape
    return pl.pallas_call(
        mix_kernel,
        grid_spec=pltpu.PrefetchScalarGridSpec(
            num_scalar_prefetch=1,
            grid=(blocks,),
            in_specs=[
                pl.BlockSpec((size, depth), lambda i, place: (place[i], 0)),
                pl.BlockSpec((depth, width), lambda i, place: (0, 0)),
            ],
            out_specs=pl.BlockSpec((size, width), lambda i, place: (i, 0)),
        ),
        out_shape=jax.ShapeDtypeStruct((blocks * size, width), BF16),
        compiler_params=pltpu.CompilerParams(vmem_limit_bytes=32 * 1024 * 1024),
        cost_estimate=pl.CostEstimate(
            flops=2 * blocks * size * depth * width,
            bytes_accessed=2 * blocks * size * width,
            transcendentals=0,
        ),
        name="mix",
    )(places, attended, weight)


def gate_kernel(x_ref, *refs):
    pieces, out_ref = refs[:-1], refs[-1]
    depth = x_ref.shape[1] // len(pieces)
    both = None
    for k, piece in enumerate(pieces):
        part = jnp.dot(
            x_ref[:, k * depth : (k + 1) * depth], piece[...], preferred_element_type=F32
        )
        both = part if both is None else both + part
    half = both.shape[1] // 2
    gate, up = both[:, :half], both[:, half:]
    out_ref[...] = (gate / (1.0 + jnp.exp(-gate)) * up).astype(BF16)


def gate_up(rows, pieces):
    size = 256
    count, depth = rows.shape
    width = pieces[0].shape[1]
    return pl.pallas_call(
        gate_kernel,
        grid=(count // size,),
        in_specs=[pl.BlockSpec((size, depth), lambda i: (i, 0))]
        + [pl.BlockSpec(piece.shape, lambda i: (0, 0)) for piece in pieces],
        out_specs=pl.BlockSpec((size, width // 2), lambda i: (i, 0)),
        out_shape=jax.ShapeDtypeStruct((count, width // 2), BF16),
        compiler_params=pltpu.CompilerParams(vmem_limit_bytes=40 * 1024 * 1024),
        cost_estimate=pl.CostEstimate(
            flops=2 * count * depth * width,
            bytes_accessed=2 * (count * depth + depth * width),
            transcendentals=count * width // 2,
        ),
        name="gate_up",
    )(rows, *pieces)


def body(
    hidden,
    request_of,
    positions,
    page_table,
    attn_gain,
    mlp_gain,
    wq,
    wk,
    wv,
    wo,
    w_gate,
    w_up,
    w_down,
):
    groups = lax.axis_size("group")
    me = lax.axis_index("tensor")
    group = lax.axis_index("group")
    odd = group % 2 == 1
    tok_group = request_of.shape[0]
    depth = hidden.shape[1]
    rows_dev = hidden.shape[0]
    places = jnp.stack([me ^ k for k in ORDER]).astype(jnp.int32)

    residual = hidden.astype(F32)
    normed = gather_rows(rms_scale(residual, attn_gain))
    small = jnp.concatenate([wq.astype(BF16), wk.astype(BF16), wv.astype(BF16)], axis=1)
    qkv_weight = lax.all_gather(small, "group", axis=0, tiled=True)
    out_weight = lax.all_gather(wo.astype(BF16), "group", axis=1, tiled=True)

    ff = w_gate.shape[1] // 2
    gate_b, up_b, down_b = w_gate.astype(BF16), w_up.astype(BF16), w_down.astype(BF16)
    lower = jnp.concatenate([gate_b[:, :ff], up_b[:, :ff]], axis=1)
    upper = jnp.concatenate([gate_b[:, ff:], up_b[:, ff:]], axis=1)
    mine_in = jnp.where(odd, upper, lower)
    other_in = jnp.where(odd, lower, upper)
    mine_out = jnp.where(odd, down_b[ff:], down_b[:ff])
    other_out = jnp.where(odd, down_b[:ff], down_b[ff:])
    in_pieces = [mine_in]
    out_pieces = [mine_out]
    for distance in range(1, groups):
        in_pieces.append(turn(mine_in if distance % 2 == 0 else other_in, distance))
    for distance in range(1, groups):
        out_pieces.append(turn(mine_out if distance % 2 == 0 else other_out, distance))

    half_dim = HD // 2
    frequency = rope_base ** (-(jnp.arange(half_dim, dtype=F32) * 2.0 / HD))
    angle = positions.astype(F32)[:, None] * frequency[None, :]
    cosine, sine = jnp.cos(angle), jnp.sin(angle)
    cosine = jnp.concatenate([cosine, cosine], axis=1)
    sine = jnp.concatenate([-sine, sine], axis=1)

    queries, kv_rows = project(normed, qkv_weight, cosine, sine, places)
    earlier = from_behind(kv_rows[-REACH:])
    attended = attend(queries, jnp.concatenate([earlier, kv_rows], axis=0), positions)
    four = len(ORDER) // 2
    mixed = residual + scatter_sum(
        mix(attended, out_weight, places[:four]), mix(attended, out_weight, places[four:])
    )
    normed_mlp = rms_scale(mixed, mlp_gain)

    def to_turned(rows):
        blocks = rows.reshape(rows.shape[0], groups, depth // groups)
        picked = [
            lax.dynamic_index_in_dim(blocks, (group - k) % groups, 1, keepdims=False)
            for k in range(groups)
        ]
        return jnp.concatenate(picked, axis=1)

    def mlp(rows):
        acts = gate_up(gather_rows(to_turned(rows)), in_pieces)
        part = jnp.concatenate(
            [jnp.dot(acts, piece, preferred_element_type=F32).astype(BF16) for piece in out_pieces],
            axis=1,
        )
        middle = part.shape[0] // 2
        summed = scatter_sum(part[:middle], part[middle:])
        return to_turned(summed)

    other_rows = pair_swap(normed_mlp)
    own_sum = mlp(normed_mlp)
    other_sum = mlp(other_rows)
    from_pair = pair_swap(other_sum.astype(BF16))
    layer_out = (mixed + own_sum + from_pair.astype(F32)).astype(BF16)

    pages = page_table.shape[1]
    changed = jnp.concatenate(
        [jnp.ones((1,), jnp.int32), (request_of[1:] != request_of[:-1]).astype(jnp.int32)]
    )
    opens = jnp.maximum(changed, (positions % PAGE == 0).astype(jnp.int32))
    logical = jnp.cumsum(opens) - 1
    chosen = jnp.sum(
        jnp.where(logical[:, None] == jnp.arange(pages)[None, :], page_table, 0), axis=1
    )
    target = chosen * PAGE + positions % PAGE
    width = kv_rows.shape[1]
    cache = jnp.zeros((pages * PAGE, width), BF16).at[target].set(kv_rows)
    return (layer_out, cache.reshape(pages, PAGE, width))


def partner(value, axis, distance):
    mask = 2**distance
    pairs = [(source, source ^ mask) for source in range(lax.axis_size(axis))]
    return lax.ppermute(value, axis, pairs)


def plain_from_behind(block, axis, distance):
    devices = range(lax.axis_size(axis))
    route = [(i - distance, i) for i in devices if i - distance in devices]
    return lax.ppermute(block, axis, route)


def plain_rms_scale(values, gain):
    square = jnp.mean(values * values, axis=-1, keepdims=True)
    return (values * lax.rsqrt(square + norm_eps) * gain).astype(jnp.bfloat16)


def rotate(values, places):
    half_dim = values.shape[-1] // 2
    frequency = rope_base ** (-(jnp.arange(half_dim, dtype=jnp.float32) * 2.0 / values.shape[-1]))
    angle = places.astype(jnp.float32)[:, None] * frequency[None, :]
    cosine = jnp.cos(angle)[:, None, :]
    sine = jnp.sin(angle)[:, None, :]
    widened = values.astype(jnp.float32)
    first = widened[..., :half_dim]
    second = widened[..., half_dim:]
    return jnp.concatenate(
        [first * cosine - second * sine, second * cosine + first * sine], axis=-1
    ).astype(jnp.bfloat16)


def join_halves(own_part, other_part):
    even = lax.axis_index("tensor") % 2 == 0
    lower = jnp.where(even, own_part, other_part)
    upper = jnp.where(even, other_part, own_part)
    return jnp.concatenate([lower, upper], axis=-1)


def contract_rows(acts, pieces):
    return tuple((jnp.dot(acts, piece, preferred_element_type=jnp.float32) for piece in pieces))


def plain_body(
    hidden,
    request_of,
    positions,
    page_table,
    attn_gain,
    mlp_gain,
    wq,
    wk,
    wv,
    wo,
    w_gate,
    w_up,
    w_down,
):
    tensor_count = lax.axis_size("tensor")
    rows_dev = hidden.shape[0]
    tok_group = request_of.shape[0]
    query_heads = QH // tensor_count
    key_heads = max(1, KVH // tensor_count)
    group_ratio = QH // KVH
    paired = tensor_count > KVH
    residual = lax.all_gather(hidden, "tensor", axis=0, tiled=True).astype(jnp.float32)
    normed = plain_rms_scale(residual, attn_gain)
    query_rows = wq.astype(jnp.bfloat16)
    key_rows = wk.astype(jnp.bfloat16)
    value_rows = wv.astype(jnp.bfloat16)
    if paired:
        other_key, other_value = partner((key_rows, value_rows), "tensor", 0)
        key_rows = join_halves(key_rows, other_key)
        value_rows = join_halves(value_rows, other_value)
    query_sum, key_sum, value_sum = contract_rows(
        normed,
        (
            lax.all_gather(query_rows, "group", axis=0, tiled=True),
            lax.all_gather(key_rows, "group", axis=0, tiled=True),
            lax.all_gather(value_rows, "group", axis=0, tiled=True),
        ),
    )
    query_raw = query_sum.astype(jnp.bfloat16)
    key_raw = key_sum.astype(jnp.bfloat16)
    value_raw = value_sum.astype(jnp.bfloat16)
    queries = rotate(query_raw.reshape(tok_group, query_heads, HD), positions)
    keys = rotate(key_raw.reshape(tok_group, key_heads, HD), positions)
    values = value_raw.reshape(tok_group, key_heads, HD)
    kv_rows = jnp.stack([keys, values], axis=2)
    earlier = plain_from_behind(kv_rows, "group", 1)
    earlier_rows = earlier.shape[0]
    all_rows = jnp.concatenate([earlier, kv_rows], axis=0)
    all_keys = jnp.repeat(all_rows[:, :, 0], group_ratio, axis=1)[:, :query_heads]
    all_values = jnp.repeat(all_rows[:, :, 1], group_ratio, axis=1)[:, :query_heads]
    first_request = request_of[0]
    first_position = positions[0]
    same_local = (request_of[:, None] == request_of[None, :]) & (
        positions[None, :] <= positions[:, None]
    )
    same_earlier = (request_of[:, None] == first_request) & (
        jnp.arange(earlier_rows)[None, :] >= earlier_rows - first_position
    )
    visible = jnp.concatenate([same_earlier, same_local], axis=1)
    scores = jnp.einsum(
        "qhd,khd->hqk", queries, all_keys, preferred_element_type=jnp.float32
    ) * HD ** (-0.5)
    scores = jnp.where(visible[None], scores, -1e30)
    row_peak = jnp.max(scores, axis=-1, keepdims=True)
    probs = jnp.where(visible[None], jnp.exp(scores - row_peak), 0.0)
    total = jnp.sum(probs, axis=-1, keepdims=True)
    mixed_heads = jnp.einsum(
        "hqk,khd->qhd", probs.astype(jnp.bfloat16), all_values, preferred_element_type=jnp.float32
    ) / jnp.transpose(total, (1, 0, 2))
    attended = mixed_heads.astype(jnp.bfloat16).reshape(tok_group, query_heads * HD)
    out_rows = wo.astype(jnp.bfloat16)
    attn_part = jnp.dot(
        attended,
        lax.all_gather(out_rows, "group", axis=1, tiled=True),
        preferred_element_type=jnp.float32,
    )
    mixed = residual + lax.psum(attn_part.astype(jnp.bfloat16), "tensor").astype(jnp.float32)
    normed_mlp = plain_rms_scale(mixed, mlp_gain)
    gate_rows = w_gate.astype(jnp.bfloat16)
    up_rows = w_up.astype(jnp.bfloat16)
    gate_sum, up_sum = contract_rows(
        normed_mlp,
        (
            lax.all_gather(gate_rows, "group", axis=0, tiled=True),
            lax.all_gather(up_rows, "group", axis=0, tiled=True),
        ),
    )
    activation = (jax.nn.silu(gate_sum) * up_sum).astype(jnp.bfloat16)
    down_rows = w_down.astype(jnp.bfloat16)
    down_part = jnp.dot(
        activation,
        lax.all_gather(down_rows, "group", axis=1, tiled=True),
        preferred_element_type=jnp.float32,
    )
    summed = lax.psum(down_part.astype(jnp.bfloat16), "tensor").astype(jnp.float32)
    first_row = lax.axis_index("tensor") * rows_dev
    own_mixed = lax.dynamic_slice_in_dim(mixed, first_row, rows_dev, 0)
    own_summed = lax.dynamic_slice_in_dim(summed, first_row, rows_dev, 0)
    layer_out = (own_mixed + own_summed).astype(jnp.bfloat16)
    pages = page_table.shape[1]
    changed = jnp.concatenate(
        [jnp.ones((1,), jnp.int32), (request_of[1:] != request_of[:-1]).astype(jnp.int32)]
    )
    opens = jnp.maximum(changed, (positions % PAGE == 0).astype(jnp.int32))
    logical = jnp.cumsum(opens) - 1
    chosen = jnp.sum(
        jnp.where(logical[:, None] == jnp.arange(pages)[None, :], page_table, 0), axis=1
    )
    target = chosen * PAGE + positions % PAGE
    width = 2 * KVH * HD // tensor_count
    flat_rows = kv_rows.reshape(tok_group, key_heads * 2 * HD)
    offset = lax.axis_index("tensor") * width % (key_heads * 2 * HD)
    own_slice = lax.dynamic_slice_in_dim(flat_rows, offset, width, 1)
    cache = jnp.zeros((pages * PAGE, width), jnp.bfloat16).at[target].set(own_slice)
    return (layer_out, cache.reshape(pages, PAGE, width))


def solution(mesh):
    shaped = mesh.shape["tensor"] == len(ORDER) and mesh.shape["group"] % 2 == 0
    placed = (
        P(("group", "tensor"), None),
        P("group"),
        P("group"),
        P("group", None),
        P(),
        P(),
        P("group", "tensor"),
        P("group", "tensor"),
        P("group", "tensor"),
        P("tensor", "group"),
        P("group", "tensor"),
        P("group", "tensor"),
        P("tensor", "group"),
    )
    return jax.shard_map(
        body if shaped else plain_body,
        mesh=mesh,
        in_specs=placed,
        out_specs=(P(("group", "tensor"), None), P("group", None, "tensor")),
        check_vma=False,
    )
```

```python
import functools

import jax
import jax.numpy as jnp
from jax import lax
from jax.experimental import pallas as pl
from jax.experimental.pallas import tpu as pltpu
from jax.sharding import PartitionSpec as P

QH = 16
KVH = 8
HD = 128
PAGE = 128
REACH = 512

rope_base = 1000000.0
norm_eps = 1e-06

F32 = jnp.float32
BF16 = jnp.bfloat16

ORDER = (2, 6, 4, 0, 3, 7, 5, 1)


def swap(value, distance):
    return lax.ppermute(
        value, "tensor", [(i, i ^ distance) for i in range(lax.axis_size("tensor"))]
    )


def turn(value, distance):
    count = lax.axis_size("group")
    return lax.ppermute(value, "group", [(i, (i + distance) % count) for i in range(count)])


def pair_swap(value):
    return lax.ppermute(value, "group", [(i, i ^ 1) for i in range(lax.axis_size("group"))])


def from_behind(block):
    count = lax.axis_size("group")
    return lax.ppermute(block, "group", [(i, i + 1) for i in range(count - 1)])


def tied(*values):
    return lax.optimization_barrier(values)


def after(value, *others):
    return lax.optimization_barrier((value, *others))[0]


def rms_scale(values, gain):
    square = jnp.mean(values * values, axis=-1, keepdims=True)
    return (values * lax.rsqrt(square + norm_eps) * gain).astype(BF16)


def gather_first(own):
    return swap(own, 2), swap(own, 4)


def gather_far(firsts):
    by_x, by_y = firsts
    half = by_x.shape[0] // 2
    return swap(by_x[:half], 4), swap(by_y[half:], 2)


def near_blocks(own, firsts, far):
    return [firsts[0], far[0], far[1], firsts[1], own]


def over(near):
    return [swap(block, 1) for block in near]


def wide_sum(*terms):
    total = terms[0].astype(F32)
    for term in terms[1:]:
        total = total + term.astype(F32)
    return total


def scatter_sum(mine, other):
    got_left, got_right = (swap(half, 1) for half in other)
    left, right = mine
    rows = left.shape[0] // 4
    two, three = 2 * rows, 3 * rows
    left_in = swap(wide_sum(left[:two], got_left[:two]).astype(BF16), 2)
    right_in = swap(wide_sum(right[rows:three], got_right[rows:three]).astype(BF16), 4)
    left_on = wide_sum(left[two:three], got_left[two:three], left_in[rows:]).astype(BF16)
    right_on = wide_sum(right[:rows], got_right[:rows], right_in[:rows]).astype(BF16)
    left_last = swap(left_on, 4)
    right_last = swap(right_on, 2)
    return (
        wide_sum(left[three:], got_left[three:], left_in[:rows], left_last),
        wide_sum(right[three:], got_right[three:], right_in[rows:], right_last),
    )


def project_kernel(blocks, places, *refs):
    rows, (w_ref, cos_ref, sin_ref, q_ref, kv_ref) = refs[:blocks], refs[blocks:]
    heads = q_ref.shape[1] // HD
    for b, block in enumerate(rows):
        size = block.shape[0]
        raw = jnp.dot(block[...], w_ref[...], preferred_element_type=F32).astype(BF16)
        here = pl.ds(pl.multiple_of(places[b], 32), size)
        cosine = cos_ref[here, :]
        sine = sin_ref[here, :]

        def rotated(head):
            wide = raw[:, head * HD : (head + 1) * HD].astype(F32)
            turned = jnp.concatenate([wide[:, HD // 2 :], wide[:, : HD // 2]], axis=1)
            return (wide * cosine + turned * sine).astype(BF16)

        for head in range(heads):
            q_ref[here, head * HD : (head + 1) * HD] = rotated(head)
        kv_ref[here, :HD] = rotated(heads)
        kv_ref[here, HD:] = raw[:, (heads + 1) * HD :]


def project(blocks, weight, cosine, sine, places):
    rows = cosine.shape[0]
    depth, width = weight.shape
    vmem = pl.BlockSpec(memory_space=pltpu.VMEM)
    smem = pl.BlockSpec(memory_space=pltpu.SMEM)
    return pl.pallas_call(
        functools.partial(project_kernel, len(blocks)),
        in_specs=[smem] + [vmem] * (len(blocks) + 3),
        out_specs=[vmem, vmem],
        out_shape=[
            jax.ShapeDtypeStruct((rows, width - 2 * HD), BF16),
            jax.ShapeDtypeStruct((rows, 2 * HD), BF16),
        ],
        compiler_params=pltpu.CompilerParams(vmem_limit_bytes=40 * 1024 * 1024),
        cost_estimate=pl.CostEstimate(
            flops=2 * rows * depth * width,
            bytes_accessed=2 * (rows * depth + depth * width),
            transcendentals=0,
        ),
        name="project",
    )(places, *blocks, weight, cosine, sine)


def attend_kernel(q_ref, kv_ref, pos_ref, out_ref):
    step = pl.program_id(0)
    size = q_ref.shape[0]
    span = size + REACH
    window = pl.ds(pl.multiple_of(step * size, size), span)
    keys = kv_ref[window, :HD]
    values = kv_ref[window, HD:]
    row = lax.broadcasted_iota(jnp.int32, (size, span), 0)
    column = lax.broadcasted_iota(jnp.int32, (size, span), 1)
    back = row + REACH - column
    visible = (back >= 0) & (back <= pos_ref[...])
    for head in range(q_ref.shape[1] // HD):
        query = q_ref[:, head * HD : (head + 1) * HD]
        scores = lax.dot_general(
            query, keys, (((1,), (1,)), ((), ())), preferred_element_type=F32
        ) * HD ** (-0.5)
        scores = jnp.where(visible, scores, -1e30)
        peak = jnp.max(scores, axis=1, keepdims=True)
        probs = jnp.exp(scores - peak)
        total = jnp.sum(probs, axis=1, keepdims=True)
        mixed = jnp.dot(probs.astype(BF16), values, preferred_element_type=F32)
        out_ref[:, head * HD : (head + 1) * HD] = (mixed / total).astype(BF16)


def attend(queries, keys_values, positions, first, last):
    size = 256
    width = queries.shape[1]
    rows = last - first
    skip = first // size
    return pl.pallas_call(
        attend_kernel,
        grid=(rows // size,),
        in_specs=[
            pl.BlockSpec((size, width), lambda i: (i + skip, 0)),
            pl.BlockSpec(keys_values.shape, lambda i: (0, 0)),
            pl.BlockSpec((size, 1), lambda i: (i + skip, 0)),
        ],
        out_specs=pl.BlockSpec((size, width), lambda i: (i, 0)),
        out_shape=jax.ShapeDtypeStruct((rows, width), BF16),
        compiler_params=pltpu.CompilerParams(vmem_limit_bytes=32 * 1024 * 1024),
        cost_estimate=pl.CostEstimate(
            flops=4 * rows * (size + REACH) * width,
            bytes_accessed=4 * rows * width,
            transcendentals=rows * (size + REACH) * width // HD,
        ),
        name="attend",
    )(queries, keys_values, positions)


def mix_kernel(rows, places, x_ref, w_ref, left_ref, right_ref):
    half = left_ref.shape[1]
    for b in range(places.shape[0]):
        block = x_ref[pl.ds(pl.multiple_of(places[b], 32), rows), :]
        total = jnp.dot(block, w_ref[...], preferred_element_type=F32).astype(BF16)
        left_ref[b * rows : (b + 1) * rows, :] = total[:, :half]
        right_ref[b * rows : (b + 1) * rows, :] = total[:, half:]


def mix(attended, weight, places, rows):
    count = places.shape[0] * rows
    depth, width = weight.shape
    vmem = pl.BlockSpec(memory_space=pltpu.VMEM)
    return pl.pallas_call(
        functools.partial(mix_kernel, rows),
        in_specs=[pl.BlockSpec(memory_space=pltpu.SMEM), vmem, vmem],
        out_specs=[vmem, vmem],
        out_shape=[jax.ShapeDtypeStruct((count, width // 2), BF16)] * 2,
        compiler_params=pltpu.CompilerParams(vmem_limit_bytes=40 * 1024 * 1024),
        cost_estimate=pl.CostEstimate(
            flops=2 * count * depth * width,
            bytes_accessed=2 * count * width,
            transcendentals=0,
        ),
        name="mix",
    )(places, attended, weight)


def gate_kernel(blocks, sources, *refs):
    rows, pieces, out_ref = refs[:blocks], refs[blocks:-1], refs[-1]
    depth = pieces[0].shape[0]
    start = 0
    for block in rows:
        both = None
        for k, piece in enumerate(pieces):
            columns = pl.ds(pl.multiple_of(sources[k] * depth, depth), depth)
            part = jnp.dot(block[:, columns], piece[...], preferred_element_type=F32)
            both = part if both is None else both + part
        half = both.shape[1] // 2
        gate, up = both[:, :half], both[:, half:]
        stop = start + block.shape[0]
        out_ref[start:stop, :] = (gate / (1.0 + jnp.exp(-gate)) * up).astype(BF16)
        start = stop


def gate_up(blocks, pieces, sources):
    count = sum(block.shape[0] for block in blocks)
    depth = blocks[0].shape[1]
    width = pieces[0].shape[1]
    vmem = pl.BlockSpec(memory_space=pltpu.VMEM)
    return pl.pallas_call(
        functools.partial(gate_kernel, len(blocks)),
        in_specs=[pl.BlockSpec(memory_space=pltpu.SMEM)] + [vmem] * (len(blocks) + len(pieces)),
        out_specs=vmem,
        out_shape=jax.ShapeDtypeStruct((count, width // 2), BF16),
        compiler_params=pltpu.CompilerParams(vmem_limit_bytes=40 * 1024 * 1024),
        cost_estimate=pl.CostEstimate(
            flops=2 * count * depth * width,
            bytes_accessed=2 * (count * depth + depth * width),
            transcendentals=count * width // 2,
        ),
        name="gate_up",
    )(sources, *blocks, *pieces)


def down_kernel(acts_ref, *refs):
    count = len(refs) // 2
    for piece, out_ref in zip(refs[:count], refs[count:]):
        out_ref[...] = jnp.dot(
            acts_ref[...], piece[...], preferred_element_type=F32
        ).astype(BF16)


def down(acts, pieces):
    rows, depth = acts.shape
    width = pieces[0].shape[1]
    vmem = pl.BlockSpec(memory_space=pltpu.VMEM)
    return pl.pallas_call(
        down_kernel,
        in_specs=[vmem] * (1 + len(pieces)),
        out_specs=[vmem] * len(pieces),
        out_shape=[jax.ShapeDtypeStruct((rows, width), BF16)] * len(pieces),
        compiler_params=pltpu.CompilerParams(vmem_limit_bytes=40 * 1024 * 1024),
        cost_estimate=pl.CostEstimate(
            flops=2 * rows * depth * width * len(pieces),
            bytes_accessed=2 * (rows + depth) * width * len(pieces),
            transcendentals=0,
        ),
        name="down",
    )(acts, *pieces)


def finish_kernel(count, sources, pair_sources, mixed_ref, *refs):
    own, pair, (out_ref, total) = refs[:count], refs[count:-2], refs[-2:]
    width = own[0].shape[1]

    def at(place):
        return pl.ds(pl.multiple_of(place * width, width), width)

    for k in range(count):
        columns = at(sources[k])
        total[:, columns] = mixed_ref[:, columns] + own[k][...]
    for k in range(count):
        columns = at(pair_sources[k])
        out_ref[:, columns] = (total[:, columns] + pair[k][...].astype(F32)).astype(BF16)


def finish(mixed, own, pair, sources, pair_sources):
    vmem = pl.BlockSpec(memory_space=pltpu.VMEM)
    smem = pl.BlockSpec(memory_space=pltpu.SMEM)
    return pl.pallas_call(
        functools.partial(finish_kernel, len(own)),
        in_specs=[smem, smem] + [vmem] * (1 + 2 * len(own)),
        out_specs=vmem,
        out_shape=jax.ShapeDtypeStruct(mixed.shape, BF16),
        scratch_shapes=[pltpu.VMEM(mixed.shape, F32)],
        compiler_params=pltpu.CompilerParams(vmem_limit_bytes=16 * 1024 * 1024),
        name="finish",
    )(sources, pair_sources, mixed, *own, *pair)


def body(
    hidden,
    request_of,
    positions,
    page_table,
    attn_gain,
    mlp_gain,
    wq,
    wk,
    wv,
    wo,
    w_gate,
    w_up,
    w_down,
):
    groups = lax.axis_size("group")
    me = lax.axis_index("tensor")
    group = lax.axis_index("group")
    odd = group % 2 == 1
    tok_group = request_of.shape[0]
    depth = hidden.shape[1]
    rows_dev = hidden.shape[0]
    sources = jnp.stack([(group - k) % groups for k in range(groups)]).astype(jnp.int32)
    pair_sources = jnp.stack([((group ^ 1) - k) % groups for k in range(groups)]).astype(jnp.int32)
    starts = []
    for k in ORDER:
        first = (me ^ k) * rows_dev
        starts += [first, first + rows_dev // 2] if k in (6, 7) else [first]
    places = jnp.stack(starts).astype(jnp.int32)

    small = jnp.concatenate([wq.astype(BF16), wk.astype(BF16), wv.astype(BF16)], axis=1)
    qkv_weight = lax.all_gather(small, "group", axis=0, tiled=True)
    own_normed = rms_scale(hidden.astype(F32), attn_gain)
    firsts = gather_first(own_normed)
    far = gather_far(firsts)
    near = near_blocks(own_normed, firsts, far)
    normed = near + over(near)
    out_weight = lax.all_gather(wo.astype(BF16), "group", axis=1, tiled=True)

    half_dim = HD // 2
    frequency = rope_base ** (-(jnp.arange(half_dim, dtype=F32) * 2.0 / HD))
    angle = positions.astype(F32)[:, None] * frequency[None, :]
    cosine, sine = jnp.cos(angle), jnp.sin(angle)
    cosine = jnp.concatenate([cosine, cosine], axis=1)
    sine = jnp.concatenate([-sine, sine], axis=1)

    queries, kv_rows = project(normed, qkv_weight, cosine, sine, places)
    earlier = from_behind(kv_rows[-REACH:])
    places_in = positions[:, None]
    late = attend(queries, kv_rows, places_in, REACH, tok_group)
    early_kv = jnp.concatenate([earlier, kv_rows[:REACH]], axis=0)
    early = attend(queries, early_kv, places_in, 0, REACH)
    attended = jnp.concatenate([early, late], axis=0)

    ff = w_gate.shape[1] // 2
    gate_b, up_b, down_b = w_gate.astype(BF16), w_up.astype(BF16), w_down.astype(BF16)
    lower = jnp.concatenate([gate_b[:, :ff], up_b[:, :ff]], axis=1)
    upper = jnp.concatenate([gate_b[:, ff:], up_b[:, ff:]], axis=1)
    mine_in = jnp.where(odd, upper, lower)
    other_in = jnp.where(odd, lower, upper)
    mine_out = jnp.where(odd, down_b[ff:], down_b[:ff])
    other_out = jnp.where(odd, down_b[:ff], down_b[ff:])
    gated_in = after(other_in, late)
    in_pieces = [mine_in] + [None] * (groups - 1)
    for distance in range(1, groups, 2):
        in_pieces[distance] = turn(gated_in, distance)

    pages = page_table.shape[1]
    changed = jnp.concatenate(
        [jnp.ones((1,), jnp.int32), (request_of[1:] != request_of[:-1]).astype(jnp.int32)]
    )
    opens = jnp.maximum(changed, (positions % PAGE == 0).astype(jnp.int32))
    logical = jnp.cumsum(opens) - 1
    chosen = jnp.sum(
        jnp.where(logical[:, None] == jnp.arange(pages)[None, :], page_table, 0), axis=1
    )
    target = chosen * PAGE + positions % PAGE
    width = kv_rows.shape[1]
    cache = jnp.zeros((pages * PAGE, width), BF16).at[target].set(kv_rows)

    four = len(ORDER) // 2
    block_places = jnp.stack([(me ^ k) * rows_dev for k in ORDER]).astype(jnp.int32)
    other = mix(attended, out_weight, block_places[four:], rows_dev)
    mine = mix(attended, out_weight, block_places[:four], rows_dev)
    sums = jnp.concatenate(scatter_sum(mine, other), axis=1)
    sums, in_pieces[1] = tied(sums, in_pieces[1])
    mixed = hidden.astype(F32) + sums
    normed_mlp = rms_scale(mixed, mlp_gain)

    other_rows = pair_swap(normed_mlp)
    firsts = gather_first(normed_mlp)
    firsts, cache, in_pieces[3], mine_in = tied(firsts, cache, in_pieces[3], mine_in)
    in_pieces[2] = turn(mine_in, 2)
    own_near = near_blocks(normed_mlp, firsts, gather_far(firsts))
    own_blocks = [own_near, over(own_near)]
    other_rows = after(other_rows, own_near)
    firsts = gather_first(other_rows)
    firsts, in_pieces[2], mine_out, other_out = tied(firsts, in_pieces[2], mine_out, other_out)
    other_near = near_blocks(other_rows, firsts, gather_far(firsts))
    other_blocks = [other_near, over(other_near)]
    out_pieces = [mine_out]
    for distance in range(1, groups):
        out_pieces.append(turn(mine_out if distance % 2 == 0 else other_out, distance))

    def acts_of(blocks):
        near, across = blocks
        return gate_up(across, in_pieces, sources), gate_up(near, in_pieces, sources)

    def sums_of(acts, pieces):
        across, near = acts
        other = down(across, pieces)
        return scatter_sum(down(near, pieces), other)

    own_acts = acts_of(own_blocks)
    other_acts = acts_of(other_blocks)
    order, own_sums, pair_sums = [], [], []
    for first, second in ((0, 1), (3, 2)):
        pieces = [out_pieces[first], out_pieces[second]]
        order += [first, second]
        pair = jnp.concatenate([half.astype(BF16) for half in sums_of(other_acts, pieces)], axis=1)
        own_sums += sums_of(own_acts, pieces)
        pair = pair_swap(pair)
        pair_sums += [pair[:, : pair.shape[1] // 2], pair[:, pair.shape[1] // 2 :]]
    order = jnp.array(order)
    layer_out = finish(mixed, own_sums, pair_sums, sources[order], pair_sources[order])
    return (layer_out, cache.reshape(pages, PAGE, width))


def partner(value, axis, distance):
    mask = 2**distance
    pairs = [(source, source ^ mask) for source in range(lax.axis_size(axis))]
    return lax.ppermute(value, axis, pairs)


def plain_from_behind(block, axis, distance):
    devices = range(lax.axis_size(axis))
    route = [(i - distance, i) for i in devices if i - distance in devices]
    return lax.ppermute(block, axis, route)


def plain_rms_scale(values, gain):
    square = jnp.mean(values * values, axis=-1, keepdims=True)
    return (values * lax.rsqrt(square + norm_eps) * gain).astype(jnp.bfloat16)


def rotate(values, places):
    half_dim = values.shape[-1] // 2
    frequency = rope_base ** (-(jnp.arange(half_dim, dtype=jnp.float32) * 2.0 / values.shape[-1]))
    angle = places.astype(jnp.float32)[:, None] * frequency[None, :]
    cosine = jnp.cos(angle)[:, None, :]
    sine = jnp.sin(angle)[:, None, :]
    widened = values.astype(jnp.float32)
    first = widened[..., :half_dim]
    second = widened[..., half_dim:]
    return jnp.concatenate(
        [first * cosine - second * sine, second * cosine + first * sine], axis=-1
    ).astype(jnp.bfloat16)


def join_halves(own_part, other_part):
    even = lax.axis_index("tensor") % 2 == 0
    lower = jnp.where(even, own_part, other_part)
    upper = jnp.where(even, other_part, own_part)
    return jnp.concatenate([lower, upper], axis=-1)


def contract_rows(acts, pieces):
    return tuple((jnp.dot(acts, piece, preferred_element_type=jnp.float32) for piece in pieces))


def plain_body(
    hidden,
    request_of,
    positions,
    page_table,
    attn_gain,
    mlp_gain,
    wq,
    wk,
    wv,
    wo,
    w_gate,
    w_up,
    w_down,
):
    tensor_count = lax.axis_size("tensor")
    rows_dev = hidden.shape[0]
    tok_group = request_of.shape[0]
    query_heads = QH // tensor_count
    key_heads = max(1, KVH // tensor_count)
    group_ratio = QH // KVH
    paired = tensor_count > KVH
    residual = lax.all_gather(hidden, "tensor", axis=0, tiled=True).astype(jnp.float32)
    normed = plain_rms_scale(residual, attn_gain)
    query_rows = wq.astype(jnp.bfloat16)
    key_rows = wk.astype(jnp.bfloat16)
    value_rows = wv.astype(jnp.bfloat16)
    if paired:
        other_key, other_value = partner((key_rows, value_rows), "tensor", 0)
        key_rows = join_halves(key_rows, other_key)
        value_rows = join_halves(value_rows, other_value)
    query_sum, key_sum, value_sum = contract_rows(
        normed,
        (
            lax.all_gather(query_rows, "group", axis=0, tiled=True),
            lax.all_gather(key_rows, "group", axis=0, tiled=True),
            lax.all_gather(value_rows, "group", axis=0, tiled=True),
        ),
    )
    query_raw = query_sum.astype(jnp.bfloat16)
    key_raw = key_sum.astype(jnp.bfloat16)
    value_raw = value_sum.astype(jnp.bfloat16)
    queries = rotate(query_raw.reshape(tok_group, query_heads, HD), positions)
    keys = rotate(key_raw.reshape(tok_group, key_heads, HD), positions)
    values = value_raw.reshape(tok_group, key_heads, HD)
    kv_rows = jnp.stack([keys, values], axis=2)
    earlier = plain_from_behind(kv_rows, "group", 1)
    earlier_rows = earlier.shape[0]
    all_rows = jnp.concatenate([earlier, kv_rows], axis=0)
    all_keys = jnp.repeat(all_rows[:, :, 0], group_ratio, axis=1)[:, :query_heads]
    all_values = jnp.repeat(all_rows[:, :, 1], group_ratio, axis=1)[:, :query_heads]
    first_request = request_of[0]
    first_position = positions[0]
    same_local = (request_of[:, None] == request_of[None, :]) & (
        positions[None, :] <= positions[:, None]
    )
    same_earlier = (request_of[:, None] == first_request) & (
        jnp.arange(earlier_rows)[None, :] >= earlier_rows - first_position
    )
    visible = jnp.concatenate([same_earlier, same_local], axis=1)
    scores = jnp.einsum(
        "qhd,khd->hqk", queries, all_keys, preferred_element_type=jnp.float32
    ) * HD ** (-0.5)
    scores = jnp.where(visible[None], scores, -1e30)
    row_peak = jnp.max(scores, axis=-1, keepdims=True)
    probs = jnp.where(visible[None], jnp.exp(scores - row_peak), 0.0)
    total = jnp.sum(probs, axis=-1, keepdims=True)
    mixed_heads = jnp.einsum(
        "hqk,khd->qhd", probs.astype(jnp.bfloat16), all_values, preferred_element_type=jnp.float32
    ) / jnp.transpose(total, (1, 0, 2))
    attended = mixed_heads.astype(jnp.bfloat16).reshape(tok_group, query_heads * HD)
    out_rows = wo.astype(jnp.bfloat16)
    attn_part = jnp.dot(
        attended,
        lax.all_gather(out_rows, "group", axis=1, tiled=True),
        preferred_element_type=jnp.float32,
    )
    mixed = residual + lax.psum(attn_part.astype(jnp.bfloat16), "tensor").astype(jnp.float32)
    normed_mlp = plain_rms_scale(mixed, mlp_gain)
    gate_rows = w_gate.astype(jnp.bfloat16)
    up_rows = w_up.astype(jnp.bfloat16)
    gate_sum, up_sum = contract_rows(
        normed_mlp,
        (
            lax.all_gather(gate_rows, "group", axis=0, tiled=True),
            lax.all_gather(up_rows, "group", axis=0, tiled=True),
        ),
    )
    activation = (jax.nn.silu(gate_sum) * up_sum).astype(jnp.bfloat16)
    down_rows = w_down.astype(jnp.bfloat16)
    down_part = jnp.dot(
        activation,
        lax.all_gather(down_rows, "group", axis=1, tiled=True),
        preferred_element_type=jnp.float32,
    )
    summed = lax.psum(down_part.astype(jnp.bfloat16), "tensor").astype(jnp.float32)
    first_row = lax.axis_index("tensor") * rows_dev
    own_mixed = lax.dynamic_slice_in_dim(mixed, first_row, rows_dev, 0)
    own_summed = lax.dynamic_slice_in_dim(summed, first_row, rows_dev, 0)
    layer_out = (own_mixed + own_summed).astype(jnp.bfloat16)
    pages = page_table.shape[1]
    changed = jnp.concatenate(
        [jnp.ones((1,), jnp.int32), (request_of[1:] != request_of[:-1]).astype(jnp.int32)]
    )
    opens = jnp.maximum(changed, (positions % PAGE == 0).astype(jnp.int32))
    logical = jnp.cumsum(opens) - 1
    chosen = jnp.sum(
        jnp.where(logical[:, None] == jnp.arange(pages)[None, :], page_table, 0), axis=1
    )
    target = chosen * PAGE + positions % PAGE
    width = 2 * KVH * HD // tensor_count
    flat_rows = kv_rows.reshape(tok_group, key_heads * 2 * HD)
    offset = lax.axis_index("tensor") * width % (key_heads * 2 * HD)
    own_slice = lax.dynamic_slice_in_dim(flat_rows, offset, width, 1)
    cache = jnp.zeros((pages * PAGE, width), jnp.bfloat16).at[target].set(own_slice)
    return (layer_out, cache.reshape(pages, PAGE, width))


def solution(mesh):
    shaped = mesh.shape["tensor"] == len(ORDER) and mesh.shape["group"] == 4
    placed = (
        P(("group", "tensor"), None),
        P("group"),
        P("group"),
        P("group", None),
        P(),
        P(),
        P("group", "tensor"),
        P("group", "tensor"),
        P("group", "tensor"),
        P("tensor", "group"),
        P("group", "tensor"),
        P("group", "tensor"),
        P("tensor", "group"),
    )
    return jax.shard_map(
        body if shaped else plain_body,
        mesh=mesh,
        in_specs=placed,
        out_specs=(P(("group", "tensor"), None), P("group", None, "tensor")),
        check_vma=False,
    )
```

```python
import functools

import jax
import jax.numpy as jnp
from jax import lax
from jax.experimental import pallas as pl
from jax.experimental.pallas import tpu as pltpu
from jax.sharding import PartitionSpec as P

QH = 16
KVH = 8
HD = 128
PAGE = 128
REACH = 512

rope_base = 1000000.0
norm_eps = 1e-06

F32 = jnp.float32
BF16 = jnp.bfloat16

ORDER = (2, 6, 4, 0, 3, 7, 5, 1)


def swap(value, distance):
    return lax.ppermute(
        value, "tensor", [(i, i ^ distance) for i in range(lax.axis_size("tensor"))]
    )


def turn(value, distance):
    count = lax.axis_size("group")
    return lax.ppermute(value, "group", [(i, (i + distance) % count) for i in range(count)])


def pair_swap(value):
    return lax.ppermute(value, "group", [(i, i ^ 1) for i in range(lax.axis_size("group"))])


def gather_alternate(value):
    count = lax.axis_size("group")
    return lax.all_gather(
        value,
        "group",
        axis=0,
        tiled=True,
        axis_index_groups=[list(range(m, count, 2)) for m in range(2)],
    )


def from_behind(block):
    count = lax.axis_size("group")
    return lax.ppermute(block, "group", [(i, i + 1) for i in range(count - 1)])


def tied(*values):
    return lax.optimization_barrier(values)


def step(started, function, *operands):
    shapes = jax.eval_shape(function, *operands)

    def nothing(*operands):
        return jax.tree.map(lambda leaf: jnp.zeros(leaf.shape, leaf.dtype), shapes)

    return lax.cond(started, function, nothing, *operands)


def after(value, *others):
    return lax.optimization_barrier((value, *others))[0]


def rms_scale(values, gain):
    square = jnp.mean(values * values, axis=-1, keepdims=True)
    return (values * lax.rsqrt(square + norm_eps) * gain).astype(BF16)


def gather_first(own):
    return swap(own, 2), swap(own, 4)


def gather_far(firsts):
    by_x, by_y = firsts
    half = by_x.shape[0] // 2
    return swap(by_x[:half], 4), swap(by_y[half:], 2)


def near_blocks(own, firsts, far):
    return [firsts[0], far[0], far[1], firsts[1], own]


def over(near):
    return [swap(block, 1) for block in near]


def wide_sum(*terms):
    total = terms[0].astype(F32)
    for term in terms[1:]:
        total = total + term.astype(F32)
    return total


def scatter_first(mine, other):
    got_left, got_right = (swap(half, 1) for half in other)
    left, right = mine
    rows = left.shape[0] // 4
    left_in = swap(wide_sum(left[: 2 * rows], got_left[: 2 * rows]).astype(BF16), 2)
    right_in = swap(wide_sum(right[rows : 3 * rows], got_right[rows : 3 * rows]).astype(BF16), 4)
    return left, right, got_left, got_right, left_in, right_in


def scatter_last(parts):
    left, right, got_left, got_right, left_in, right_in = parts
    rows = left.shape[0] // 4
    two, three = 2 * rows, 3 * rows
    left_on = wide_sum(left[two:three], got_left[two:three], left_in[rows:]).astype(BF16)
    right_on = wide_sum(right[:rows], got_right[:rows], right_in[:rows]).astype(BF16)
    left_last = swap(left_on, 4)
    right_last = swap(right_on, 2)
    return jnp.concatenate(
        [
            wide_sum(left[three:], got_left[three:], left_in[:rows], left_last),
            wide_sum(right[three:], got_right[three:], right_in[rows:], right_last),
        ],
        axis=1,
    )


def project_kernel(blocks, places, *refs):
    rows, (w_ref, cos_ref, sin_ref, q_ref, kv_ref) = refs[:blocks], refs[blocks:]
    heads = q_ref.shape[1] // HD
    for b, block in enumerate(rows):
        size = block.shape[0]
        raw = jnp.dot(block[...], w_ref[...], preferred_element_type=F32).astype(BF16)
        here = pl.ds(pl.multiple_of(places[b], 32), size)
        cosine = cos_ref[here, :]
        sine = sin_ref[here, :]

        def rotated(head):
            wide = raw[:, head * HD : (head + 1) * HD].astype(F32)
            turned = jnp.concatenate([wide[:, HD // 2 :], wide[:, : HD // 2]], axis=1)
            return (wide * cosine + turned * sine).astype(BF16)

        for head in range(heads):
            q_ref[here, head * HD : (head + 1) * HD] = rotated(head)
        kv_ref[here, :HD] = rotated(heads)
        kv_ref[here, HD:] = raw[:, (heads + 1) * HD :]


def project(blocks, weight, cosine, sine, places):
    rows = cosine.shape[0]
    depth, width = weight.shape
    vmem = pl.BlockSpec(memory_space=pltpu.VMEM)
    smem = pl.BlockSpec(memory_space=pltpu.SMEM)
    return pl.pallas_call(
        functools.partial(project_kernel, len(blocks)),
        in_specs=[smem] + [vmem] * (len(blocks) + 3),
        out_specs=[vmem, vmem],
        out_shape=[
            jax.ShapeDtypeStruct((rows, width - 2 * HD), BF16),
            jax.ShapeDtypeStruct((rows, 2 * HD), BF16),
        ],
        compiler_params=pltpu.CompilerParams(vmem_limit_bytes=40 * 1024 * 1024),
        cost_estimate=pl.CostEstimate(
            flops=2 * rows * depth * width,
            bytes_accessed=2 * (rows * depth + depth * width),
            transcendentals=0,
        ),
        name="project",
    )(places, *blocks, weight, cosine, sine)


def attend_kernel(q_ref, kv_ref, pos_ref, out_ref):
    step = pl.program_id(0)
    size = q_ref.shape[0]
    span = size + REACH
    window = pl.ds(pl.multiple_of(step * size, size), span)
    keys = kv_ref[window, :HD]
    values = kv_ref[window, HD:]
    row = lax.broadcasted_iota(jnp.int32, (size, span), 0)
    column = lax.broadcasted_iota(jnp.int32, (size, span), 1)
    back = row + REACH - column
    visible = (back >= 0) & (back <= pos_ref[...])
    for head in range(q_ref.shape[1] // HD):
        query = q_ref[:, head * HD : (head + 1) * HD]
        scores = lax.dot_general(
            query, keys, (((1,), (1,)), ((), ())), preferred_element_type=F32
        ) * HD ** (-0.5)
        scores = jnp.where(visible, scores, -1e30)
        peak = jnp.max(scores, axis=1, keepdims=True)
        probs = jnp.exp(scores - peak)
        total = jnp.sum(probs, axis=1, keepdims=True)
        mixed = jnp.dot(probs.astype(BF16), values, preferred_element_type=F32)
        out_ref[:, head * HD : (head + 1) * HD] = (mixed / total).astype(BF16)


def attend(queries, keys_values, positions, first, last):
    size = 256
    width = queries.shape[1]
    rows = last - first
    skip = first // size
    return pl.pallas_call(
        attend_kernel,
        grid=(rows // size,),
        in_specs=[
            pl.BlockSpec((size, width), lambda i: (i + skip, 0)),
            pl.BlockSpec(keys_values.shape, lambda i: (0, 0)),
            pl.BlockSpec((size, 1), lambda i: (i + skip, 0)),
        ],
        out_specs=pl.BlockSpec((size, width), lambda i: (i, 0)),
        out_shape=jax.ShapeDtypeStruct((rows, width), BF16),
        compiler_params=pltpu.CompilerParams(vmem_limit_bytes=32 * 1024 * 1024),
        cost_estimate=pl.CostEstimate(
            flops=4 * rows * (size + REACH) * width,
            bytes_accessed=4 * rows * width,
            transcendentals=rows * (size + REACH) * width // HD,
        ),
        name="attend",
    )(queries, keys_values, positions)


def mix_kernel(rows, places, x_ref, w_ref, left_ref, right_ref):
    half = left_ref.shape[1]
    for b in range(places.shape[0]):
        block = x_ref[pl.ds(pl.multiple_of(places[b], 32), rows), :]
        total = jnp.dot(block, w_ref[...], preferred_element_type=F32).astype(BF16)
        left_ref[b * rows : (b + 1) * rows, :] = total[:, :half]
        right_ref[b * rows : (b + 1) * rows, :] = total[:, half:]


def mix(attended, weight, places, rows):
    count = places.shape[0] * rows
    depth, width = weight.shape
    vmem = pl.BlockSpec(memory_space=pltpu.VMEM)
    return pl.pallas_call(
        functools.partial(mix_kernel, rows),
        in_specs=[pl.BlockSpec(memory_space=pltpu.SMEM), vmem, vmem],
        out_specs=[vmem, vmem],
        out_shape=[jax.ShapeDtypeStruct((count, width // 2), BF16)] * 2,
        compiler_params=pltpu.CompilerParams(vmem_limit_bytes=40 * 1024 * 1024),
        cost_estimate=pl.CostEstimate(
            flops=2 * count * depth * width,
            bytes_accessed=2 * count * width,
            transcendentals=0,
        ),
        name="mix",
    )(places, attended, weight)


def gate_kernel(blocks, sources, *refs):
    rows, pieces, out_ref = refs[:blocks], refs[blocks:-1], refs[-1]
    depth = rows[0].shape[1] // sources.shape[0]
    slices = [
        (piece, at) for piece in pieces for at in range(0, piece.shape[0], depth)
    ]
    start = 0
    for block in rows:
        both = None
        for k, (piece, at) in enumerate(slices):
            columns = pl.ds(pl.multiple_of(sources[k] * depth, depth), depth)
            part = jnp.dot(
                block[:, columns], piece[at : at + depth, :], preferred_element_type=F32
            )
            both = part if both is None else both + part
        half = both.shape[1] // 2
        gate, up = both[:, :half], both[:, half:]
        stop = start + block.shape[0]
        out_ref[start:stop, :] = (gate / (1.0 + jnp.exp(-gate)) * up).astype(BF16)
        start = stop


def gate_up(blocks, pieces, sources):
    count = sum(block.shape[0] for block in blocks)
    depth = blocks[0].shape[1]
    width = pieces[0].shape[1]
    vmem = pl.BlockSpec(memory_space=pltpu.VMEM)
    return pl.pallas_call(
        functools.partial(gate_kernel, len(blocks)),
        in_specs=[pl.BlockSpec(memory_space=pltpu.SMEM)] + [vmem] * (len(blocks) + len(pieces)),
        out_specs=vmem,
        out_shape=jax.ShapeDtypeStruct((count, width // 2), BF16),
        compiler_params=pltpu.CompilerParams(vmem_limit_bytes=40 * 1024 * 1024),
        cost_estimate=pl.CostEstimate(
            flops=2 * count * depth * width,
            bytes_accessed=2 * (count * depth + depth * width),
            transcendentals=count * width // 2,
        ),
        name="gate_up",
    )(sources, *blocks, *pieces)


def down_kernel(acts_ref, *refs):
    pieces, halves = refs[:-2], refs[-2:]
    depth = acts_ref.shape[1]
    width = pieces[0].shape[1]
    slices = [(piece, at) for piece in pieces for at in range(0, piece.shape[0], depth)]
    for k, (piece, at) in enumerate(slices):
        place = k % 2 * width
        halves[k // 2][:, place : place + width] = jnp.dot(
            acts_ref[...], piece[at : at + depth, :], preferred_element_type=F32
        ).astype(BF16)


def down(acts, pieces):
    rows, depth = acts.shape
    width = pieces[0].shape[1] * sum(piece.shape[0] for piece in pieces) // depth // 2
    vmem = pl.BlockSpec(memory_space=pltpu.VMEM)
    return pl.pallas_call(
        down_kernel,
        in_specs=[vmem] * (1 + len(pieces)),
        out_specs=[vmem, vmem],
        out_shape=[jax.ShapeDtypeStruct((rows, width), BF16)] * 2,
        compiler_params=pltpu.CompilerParams(vmem_limit_bytes=40 * 1024 * 1024),
        cost_estimate=pl.CostEstimate(
            flops=4 * rows * depth * width,
            bytes_accessed=4 * (rows + depth) * width,
            transcendentals=0,
        ),
        name="down",
    )(acts, *pieces)


def finish_kernel(sources, pair_sources, mixed_ref, own_ref, pair_ref, out_ref, total):
    count = sources.shape[0]
    width = mixed_ref.shape[1] // count

    def at(place):
        return pl.ds(pl.multiple_of(place * width, width), width)

    for k in range(count):
        columns = at(sources[k])
        total[:, columns] = mixed_ref[:, columns] + own_ref[:, k * width : (k + 1) * width]
    for k in range(count):
        columns = at(pair_sources[k])
        pair = pair_ref[:, k * width : (k + 1) * width].astype(F32)
        out_ref[:, columns] = (total[:, columns] + pair).astype(BF16)


def finish(mixed, own, pair, sources, pair_sources):
    vmem = pl.BlockSpec(memory_space=pltpu.VMEM)
    smem = pl.BlockSpec(memory_space=pltpu.SMEM)
    return pl.pallas_call(
        finish_kernel,
        in_specs=[smem, smem, vmem, vmem, vmem],
        out_specs=vmem,
        out_shape=jax.ShapeDtypeStruct(mixed.shape, BF16),
        scratch_shapes=[pltpu.VMEM(mixed.shape, F32)],
        compiler_params=pltpu.CompilerParams(vmem_limit_bytes=16 * 1024 * 1024),
        name="finish",
    )(sources, pair_sources, mixed, own, pair)


def body(
    hidden,
    request_of,
    positions,
    page_table,
    attn_gain,
    mlp_gain,
    wq,
    wk,
    wv,
    wo,
    w_gate,
    w_up,
    w_down,
):
    groups = lax.axis_size("group")
    me = lax.axis_index("tensor")
    group = lax.axis_index("group")
    odd = group % 2 == 1
    tok_group = request_of.shape[0]
    depth = hidden.shape[1]
    rows_dev = hidden.shape[0]
    def order_of(plane):
        alike = [plane % 2 + k for k in range(0, groups, 2)]
        return jnp.stack(alike + [(plane - k) % groups for k in (1, 3)]).astype(jnp.int32)

    sources, pair_sources = order_of(group), order_of(group ^ 1)
    starts = []
    for k in ORDER:
        first = (me ^ k) * rows_dev
        starts += [first, first + rows_dev // 2] if k in (6, 7) else [first]
    places = jnp.stack(starts).astype(jnp.int32)

    small = jnp.concatenate([wq.astype(BF16), wk.astype(BF16), wv.astype(BF16)], axis=1)
    qkv_weight = lax.all_gather(small, "group", axis=0, tiled=True)
    own_normed = rms_scale(hidden.astype(F32), attn_gain)
    firsts = gather_first(own_normed)
    ff = w_gate.shape[1] // 2
    gate_b, up_b, down_b = w_gate.astype(BF16), w_up.astype(BF16), w_down.astype(BF16)
    lower = jnp.concatenate([gate_b[:, :ff], up_b[:, :ff]], axis=1)
    upper = jnp.concatenate([gate_b[:, ff:], up_b[:, ff:]], axis=1)
    mine_in = jnp.where(odd, upper, lower)
    other_in = jnp.where(odd, lower, upper)
    mine_out = jnp.where(odd, down_b[ff:], down_b[:ff])
    other_out = jnp.where(odd, down_b[:ff], down_b[ff:])
    firsts, mine_in, other_in, mine_out, other_out = tied(
        firsts, mine_in, other_in, mine_out, other_out
    )
    far = gather_far(firsts)
    near = near_blocks(own_normed, firsts, far)
    normed = near + over(near)
    out_weight = lax.all_gather(wo.astype(BF16), "group", axis=1, tiled=True)

    half_dim = HD // 2
    frequency = rope_base ** (-(jnp.arange(half_dim, dtype=F32) * 2.0 / HD))
    angle = positions.astype(F32)[:, None] * frequency[None, :]
    cosine, sine = jnp.cos(angle), jnp.sin(angle)
    cosine = jnp.concatenate([cosine, cosine], axis=1)
    sine = jnp.concatenate([-sine, sine], axis=1)

    queries, kv_rows = project(normed, qkv_weight, cosine, sine, places)
    earlier = from_behind(kv_rows[-REACH:])
    places_in = positions[:, None]
    late = attend(queries, kv_rows, places_in, REACH, tok_group)
    early_kv = jnp.concatenate([earlier, kv_rows[:REACH]], axis=0)
    early = attend(queries, early_kv, places_in, 0, REACH)
    attended = jnp.concatenate([early, late], axis=0)

    started = positions[0] >= 0

    alike_in = gather_alternate(after(mine_in, kv_rows))

    pages = page_table.shape[1]
    changed = jnp.concatenate(
        [jnp.ones((1,), jnp.int32), (request_of[1:] != request_of[:-1]).astype(jnp.int32)]
    )
    opens = jnp.maximum(changed, (positions % PAGE == 0).astype(jnp.int32))
    logical = jnp.cumsum(opens) - 1
    chosen = jnp.sum(
        jnp.where(logical[:, None] == jnp.arange(pages)[None, :], page_table, 0), axis=1
    )
    target = chosen * PAGE + positions % PAGE
    width = kv_rows.shape[1]

    four = len(ORDER) // 2
    block_places = jnp.stack([(me ^ k) * rows_dev for k in ORDER]).astype(jnp.int32)

    def through_attention(attended, out_weight, block_places, hidden, gain):
        other = mix(attended, out_weight, block_places[four:], rows_dev)
        mine = mix(attended, out_weight, block_places[:four], rows_dev)
        mixed = hidden.astype(F32) + scatter_last(scatter_first(mine, other))
        return mixed, rms_scale(mixed, gain)

    mixed, normed_mlp = step(
        started, through_attention, attended, out_weight, block_places, hidden, mlp_gain
    )
    normed_mlp, alike_in = tied(normed_mlp, alike_in)
    alike_out = gather_alternate(after(mine_out, alike_in))

    def both_groups(own_rows, other_in, target, kv_rows):
        pair_rows = pair_swap(own_rows)
        firsts = gather_first(own_rows)
        cache = jnp.zeros((pages * PAGE, kv_rows.shape[1]), BF16).at[target].set(kv_rows)
        firsts, cache = tied(firsts, cache)
        own_near = near_blocks(own_rows, firsts, gather_far(firsts))
        own_blocks = [own_near, over(own_near)]
        near_in = turn(after(other_in, own_near), 1)
        firsts = gather_first(after(pair_rows, own_near))
        firsts, near_in = tied(firsts, near_in)
        far_in = turn(after(other_in, near_in), 3)
        pair_near = near_blocks(pair_rows, firsts, gather_far(firsts))
        return own_blocks, [pair_near, over(pair_near)], near_in, far_in, cache

    own_blocks, other_blocks, near_in, far_in, cache = step(
        started, both_groups, normed_mlp, other_in, target, kv_rows
    )
    in_pieces = [alike_in, near_in, far_in]
    own_blocks, alike_out = tied(own_blocks, alike_out)
    other_out = after(other_out, far_in)
    out_pieces = [alike_out, turn(other_out, 1), turn(other_out, 3)]

    def acts_of(blocks):
        near, across = blocks
        return gate_up(across, in_pieces, sources), gate_up(near, in_pieces, sources)

    own_acts = acts_of(own_blocks)
    other_acts = acts_of(other_blocks)
    own_acts, other_acts, out_pieces[1:] = tied(own_acts, other_acts, out_pieces[1:])

    other, mine = (down(half, out_pieces) for half in other_acts)
    pair_parts = scatter_first(mine, other)
    other, mine = (down(half, out_pieces) for half in own_acts)
    other, mine = after((other, mine), pair_parts)
    own_parts = scatter_first(mine, other)
    pair_sum = scatter_last(pair_parts).astype(BF16)
    from_pair = pair_swap(pair_sum)
    own_parts = after(own_parts, pair_sum)
    own_sum = scatter_last(own_parts)
    layer_out = finish(mixed, own_sum, from_pair, sources, pair_sources)
    return (layer_out, cache.reshape(pages, PAGE, width))


def partner(value, axis, distance):
    mask = 2**distance
    pairs = [(source, source ^ mask) for source in range(lax.axis_size(axis))]
    return lax.ppermute(value, axis, pairs)


def plain_from_behind(block, axis, distance):
    devices = range(lax.axis_size(axis))
    route = [(i - distance, i) for i in devices if i - distance in devices]
    return lax.ppermute(block, axis, route)


def plain_rms_scale(values, gain):
    square = jnp.mean(values * values, axis=-1, keepdims=True)
    return (values * lax.rsqrt(square + norm_eps) * gain).astype(jnp.bfloat16)


def rotate(values, places):
    half_dim = values.shape[-1] // 2
    frequency = rope_base ** (-(jnp.arange(half_dim, dtype=jnp.float32) * 2.0 / values.shape[-1]))
    angle = places.astype(jnp.float32)[:, None] * frequency[None, :]
    cosine = jnp.cos(angle)[:, None, :]
    sine = jnp.sin(angle)[:, None, :]
    widened = values.astype(jnp.float32)
    first = widened[..., :half_dim]
    second = widened[..., half_dim:]
    return jnp.concatenate(
        [first * cosine - second * sine, second * cosine + first * sine], axis=-1
    ).astype(jnp.bfloat16)


def join_halves(own_part, other_part):
    even = lax.axis_index("tensor") % 2 == 0
    lower = jnp.where(even, own_part, other_part)
    upper = jnp.where(even, other_part, own_part)
    return jnp.concatenate([lower, upper], axis=-1)


def contract_rows(acts, pieces):
    return tuple((jnp.dot(acts, piece, preferred_element_type=jnp.float32) for piece in pieces))


def plain_body(
    hidden,
    request_of,
    positions,
    page_table,
    attn_gain,
    mlp_gain,
    wq,
    wk,
    wv,
    wo,
    w_gate,
    w_up,
    w_down,
):
    tensor_count = lax.axis_size("tensor")
    rows_dev = hidden.shape[0]
    tok_group = request_of.shape[0]
    query_heads = QH // tensor_count
    key_heads = max(1, KVH // tensor_count)
    group_ratio = QH // KVH
    paired = tensor_count > KVH
    residual = lax.all_gather(hidden, "tensor", axis=0, tiled=True).astype(jnp.float32)
    normed = plain_rms_scale(residual, attn_gain)
    query_rows = wq.astype(jnp.bfloat16)
    key_rows = wk.astype(jnp.bfloat16)
    value_rows = wv.astype(jnp.bfloat16)
    if paired:
        other_key, other_value = partner((key_rows, value_rows), "tensor", 0)
        key_rows = join_halves(key_rows, other_key)
        value_rows = join_halves(value_rows, other_value)
    query_sum, key_sum, value_sum = contract_rows(
        normed,
        (
            lax.all_gather(query_rows, "group", axis=0, tiled=True),
            lax.all_gather(key_rows, "group", axis=0, tiled=True),
            lax.all_gather(value_rows, "group", axis=0, tiled=True),
        ),
    )
    query_raw = query_sum.astype(jnp.bfloat16)
    key_raw = key_sum.astype(jnp.bfloat16)
    value_raw = value_sum.astype(jnp.bfloat16)
    queries = rotate(query_raw.reshape(tok_group, query_heads, HD), positions)
    keys = rotate(key_raw.reshape(tok_group, key_heads, HD), positions)
    values = value_raw.reshape(tok_group, key_heads, HD)
    kv_rows = jnp.stack([keys, values], axis=2)
    earlier = plain_from_behind(kv_rows, "group", 1)
    earlier_rows = earlier.shape[0]
    all_rows = jnp.concatenate([earlier, kv_rows], axis=0)
    all_keys = jnp.repeat(all_rows[:, :, 0], group_ratio, axis=1)[:, :query_heads]
    all_values = jnp.repeat(all_rows[:, :, 1], group_ratio, axis=1)[:, :query_heads]
    first_request = request_of[0]
    first_position = positions[0]
    same_local = (request_of[:, None] == request_of[None, :]) & (
        positions[None, :] <= positions[:, None]
    )
    same_earlier = (request_of[:, None] == first_request) & (
        jnp.arange(earlier_rows)[None, :] >= earlier_rows - first_position
    )
    visible = jnp.concatenate([same_earlier, same_local], axis=1)
    scores = jnp.einsum(
        "qhd,khd->hqk", queries, all_keys, preferred_element_type=jnp.float32
    ) * HD ** (-0.5)
    scores = jnp.where(visible[None], scores, -1e30)
    row_peak = jnp.max(scores, axis=-1, keepdims=True)
    probs = jnp.where(visible[None], jnp.exp(scores - row_peak), 0.0)
    total = jnp.sum(probs, axis=-1, keepdims=True)
    mixed_heads = jnp.einsum(
        "hqk,khd->qhd", probs.astype(jnp.bfloat16), all_values, preferred_element_type=jnp.float32
    ) / jnp.transpose(total, (1, 0, 2))
    attended = mixed_heads.astype(jnp.bfloat16).reshape(tok_group, query_heads * HD)
    out_rows = wo.astype(jnp.bfloat16)
    attn_part = jnp.dot(
        attended,
        lax.all_gather(out_rows, "group", axis=1, tiled=True),
        preferred_element_type=jnp.float32,
    )
    mixed = residual + lax.psum(attn_part.astype(jnp.bfloat16), "tensor").astype(jnp.float32)
    normed_mlp = plain_rms_scale(mixed, mlp_gain)
    gate_rows = w_gate.astype(jnp.bfloat16)
    up_rows = w_up.astype(jnp.bfloat16)
    gate_sum, up_sum = contract_rows(
        normed_mlp,
        (
            lax.all_gather(gate_rows, "group", axis=0, tiled=True),
            lax.all_gather(up_rows, "group", axis=0, tiled=True),
        ),
    )
    activation = (jax.nn.silu(gate_sum) * up_sum).astype(jnp.bfloat16)
    down_rows = w_down.astype(jnp.bfloat16)
    down_part = jnp.dot(
        activation,
        lax.all_gather(down_rows, "group", axis=1, tiled=True),
        preferred_element_type=jnp.float32,
    )
    summed = lax.psum(down_part.astype(jnp.bfloat16), "tensor").astype(jnp.float32)
    first_row = lax.axis_index("tensor") * rows_dev
    own_mixed = lax.dynamic_slice_in_dim(mixed, first_row, rows_dev, 0)
    own_summed = lax.dynamic_slice_in_dim(summed, first_row, rows_dev, 0)
    layer_out = (own_mixed + own_summed).astype(jnp.bfloat16)
    pages = page_table.shape[1]
    changed = jnp.concatenate(
        [jnp.ones((1,), jnp.int32), (request_of[1:] != request_of[:-1]).astype(jnp.int32)]
    )
    opens = jnp.maximum(changed, (positions % PAGE == 0).astype(jnp.int32))
    logical = jnp.cumsum(opens) - 1
    chosen = jnp.sum(
        jnp.where(logical[:, None] == jnp.arange(pages)[None, :], page_table, 0), axis=1
    )
    target = chosen * PAGE + positions % PAGE
    width = 2 * KVH * HD // tensor_count
    flat_rows = kv_rows.reshape(tok_group, key_heads * 2 * HD)
    offset = lax.axis_index("tensor") * width % (key_heads * 2 * HD)
    own_slice = lax.dynamic_slice_in_dim(flat_rows, offset, width, 1)
    cache = jnp.zeros((pages * PAGE, width), jnp.bfloat16).at[target].set(own_slice)
    return (layer_out, cache.reshape(pages, PAGE, width))


def solution(mesh):
    shaped = mesh.shape["tensor"] == len(ORDER) and mesh.shape["group"] == 4
    placed = (
        P(("group", "tensor"), None),
        P("group"),
        P("group"),
        P("group", None),
        P(),
        P(),
        P("group", "tensor"),
        P("group", "tensor"),
        P("group", "tensor"),
        P("tensor", "group"),
        P("group", "tensor"),
        P("group", "tensor"),
        P("tensor", "group"),
    )
    return jax.shard_map(
        body if shaped else plain_body,
        mesh=mesh,
        in_specs=placed,
        out_specs=(P(("group", "tensor"), None), P("group", None, "tensor")),
        check_vma=False,
    )
```

```python
import functools

import jax
import jax.numpy as jnp
from jax import lax
from jax.experimental import pallas as pl
from jax.experimental.pallas import tpu as pltpu
from jax.sharding import PartitionSpec as P

QH = 16
KVH = 8
HD = 128
PAGE = 128
REACH = 512

rope_base = 1000000.0
norm_eps = 1e-06

F32 = jnp.float32
BF16 = jnp.bfloat16

ORDER = (2, 6, 4, 0, 3, 7, 5, 1)


def swap(value, distance):
    return lax.ppermute(
        value, "tensor", [(i, i ^ distance) for i in range(lax.axis_size("tensor"))]
    )


def turn(value, distance):
    count = lax.axis_size("group")
    return lax.ppermute(value, "group", [(i, (i + distance) % count) for i in range(count)])


def pair_swap(value):
    return lax.ppermute(value, "group", [(i, i ^ 1) for i in range(lax.axis_size("group"))])


def gather_alternate(value):
    count = lax.axis_size("group")
    return lax.all_gather(
        value,
        "group",
        axis=0,
        tiled=True,
        axis_index_groups=[list(range(m, count, 2)) for m in range(2)],
    )


def from_behind(block):
    count = lax.axis_size("group")
    return lax.ppermute(block, "group", [(i, i + 1) for i in range(count - 1)])


def tied(*values):
    return lax.optimization_barrier(values)


def step(started, function, *operands):
    shapes = jax.eval_shape(function, *operands)

    def nothing(*operands):
        return jax.tree.map(lambda leaf: jnp.zeros(leaf.shape, leaf.dtype), shapes)

    return lax.cond(started, function, nothing, *operands)


def after(value, *others):
    return lax.optimization_barrier((value, *others))[0]


def rms_scale(values, gain):
    square = jnp.mean(values * values, axis=-1, keepdims=True)
    return (values * lax.rsqrt(square + norm_eps) * gain).astype(BF16)


def gather_first(own):
    return swap(own, 2), swap(own, 4)


def gather_far(firsts):
    by_x, by_y = firsts
    half = by_x.shape[0] // 2
    return swap(by_x[:half], 4), swap(by_y[half:], 2)


def near_blocks(own, firsts, far):
    return [firsts[0], far[0], far[1], firsts[1], own]


def over(near):
    return [swap(block, 1) for block in near]


def wide_sum(*terms):
    total = terms[0].astype(F32)
    for term in terms[1:]:
        total = total + term.astype(F32)
    return total


def scatter_first(mine, other):
    got_left, got_right = (swap(half, 1) for half in other)
    left, right = mine
    rows = left.shape[0] // 4
    left_in = swap(wide_sum(left[: 2 * rows], got_left[: 2 * rows]).astype(BF16), 2)
    right_in = swap(wide_sum(right[rows : 3 * rows], got_right[rows : 3 * rows]).astype(BF16), 4)
    return left, right, got_left, got_right, left_in, right_in


def scatter_last(parts):
    left, right, got_left, got_right, left_in, right_in = parts
    rows = left.shape[0] // 4
    two, three = 2 * rows, 3 * rows
    left_on = wide_sum(left[two:three], got_left[two:three], left_in[rows:]).astype(BF16)
    right_on = wide_sum(right[:rows], got_right[:rows], right_in[:rows]).astype(BF16)
    left_last = swap(left_on, 4)
    right_last = swap(right_on, 2)
    return jnp.concatenate(
        [
            wide_sum(left[three:], got_left[three:], left_in[:rows], left_last),
            wide_sum(right[three:], got_right[three:], right_in[rows:], right_last),
        ],
        axis=1,
    )


def project_kernel(blocks, places, *refs):
    rows, (w_ref, cos_ref, sin_ref, q_ref, kv_ref) = refs[:blocks], refs[blocks:]
    heads = q_ref.shape[1] // HD
    for b, block in enumerate(rows):
        size = block.shape[0]
        raw = jnp.dot(block[...], w_ref[...], preferred_element_type=F32).astype(BF16)
        here = pl.ds(pl.multiple_of(places[b], 32), size)
        cosine = cos_ref[here, :]
        sine = sin_ref[here, :]

        def rotated(head):
            wide = raw[:, head * HD : (head + 1) * HD].astype(F32)
            turned = jnp.concatenate([wide[:, HD // 2 :], wide[:, : HD // 2]], axis=1)
            return (wide * cosine + turned * sine).astype(BF16)

        for head in range(heads):
            q_ref[here, head * HD : (head + 1) * HD] = rotated(head)
        kv_ref[here, :HD] = rotated(heads)
        kv_ref[here, HD:] = raw[:, (heads + 1) * HD :]


def project(blocks, weight, cosine, sine, places):
    rows = cosine.shape[0]
    depth, width = weight.shape
    vmem = pl.BlockSpec(memory_space=pltpu.VMEM)
    smem = pl.BlockSpec(memory_space=pltpu.SMEM)
    return pl.pallas_call(
        functools.partial(project_kernel, len(blocks)),
        in_specs=[smem] + [vmem] * (len(blocks) + 3),
        out_specs=[vmem, vmem],
        out_shape=[
            jax.ShapeDtypeStruct((rows, width - 2 * HD), BF16),
            jax.ShapeDtypeStruct((rows, 2 * HD), BF16),
        ],
        compiler_params=pltpu.CompilerParams(vmem_limit_bytes=40 * 1024 * 1024),
        cost_estimate=pl.CostEstimate(
            flops=2 * rows * depth * width,
            bytes_accessed=2 * (rows * depth + depth * width),
            transcendentals=0,
        ),
        name="project",
    )(places, *blocks, weight, cosine, sine)


def attend_kernel(q_ref, kv_ref, pos_ref, out_ref):
    step = pl.program_id(0)
    size = q_ref.shape[0]
    span = size + REACH
    window = pl.ds(pl.multiple_of(step * size, size), span)
    keys = kv_ref[window, :HD]
    values = kv_ref[window, HD:]
    row = lax.broadcasted_iota(jnp.int32, (size, span), 0)
    column = lax.broadcasted_iota(jnp.int32, (size, span), 1)
    back = row + REACH - column
    visible = (back >= 0) & (back <= pos_ref[...])
    for head in range(q_ref.shape[1] // HD):
        query = q_ref[:, head * HD : (head + 1) * HD]
        scores = lax.dot_general(
            query, keys, (((1,), (1,)), ((), ())), preferred_element_type=F32
        ) * HD ** (-0.5)
        scores = jnp.where(visible, scores, -1e30)
        peak = jnp.max(scores, axis=1, keepdims=True)
        probs = jnp.exp(scores - peak)
        total = jnp.sum(probs, axis=1, keepdims=True)
        mixed = jnp.dot(probs.astype(BF16), values, preferred_element_type=F32)
        out_ref[:, head * HD : (head + 1) * HD] = (mixed / total).astype(BF16)


def attend(queries, keys_values, positions, first, last):
    size = 256
    width = queries.shape[1]
    rows = last - first
    skip = first // size
    return pl.pallas_call(
        attend_kernel,
        grid=(rows // size,),
        in_specs=[
            pl.BlockSpec((size, width), lambda i: (i + skip, 0)),
            pl.BlockSpec(keys_values.shape, lambda i: (0, 0)),
            pl.BlockSpec((size, 1), lambda i: (i + skip, 0)),
        ],
        out_specs=pl.BlockSpec((size, width), lambda i: (i, 0)),
        out_shape=jax.ShapeDtypeStruct((rows, width), BF16),
        compiler_params=pltpu.CompilerParams(vmem_limit_bytes=32 * 1024 * 1024),
        cost_estimate=pl.CostEstimate(
            flops=4 * rows * (size + REACH) * width,
            bytes_accessed=4 * rows * width,
            transcendentals=rows * (size + REACH) * width // HD,
        ),
        name="attend",
    )(queries, keys_values, positions)


def mix_kernel(rows, places, x_ref, w_ref, left_ref, right_ref):
    half = left_ref.shape[1]
    for b in range(places.shape[0]):
        block = x_ref[pl.ds(pl.multiple_of(places[b], 32), rows), :]
        total = jnp.dot(block, w_ref[...], preferred_element_type=F32).astype(BF16)
        left_ref[b * rows : (b + 1) * rows, :] = total[:, :half]
        right_ref[b * rows : (b + 1) * rows, :] = total[:, half:]


def mix(attended, weight, places, rows):
    count = places.shape[0] * rows
    depth, width = weight.shape
    vmem = pl.BlockSpec(memory_space=pltpu.VMEM)
    return pl.pallas_call(
        functools.partial(mix_kernel, rows),
        in_specs=[pl.BlockSpec(memory_space=pltpu.SMEM), vmem, vmem],
        out_specs=[vmem, vmem],
        out_shape=[jax.ShapeDtypeStruct((count, width // 2), BF16)] * 2,
        compiler_params=pltpu.CompilerParams(vmem_limit_bytes=40 * 1024 * 1024),
        cost_estimate=pl.CostEstimate(
            flops=2 * count * depth * width,
            bytes_accessed=2 * count * width,
            transcendentals=0,
        ),
        name="mix",
    )(places, attended, weight)


def gate_kernel(blocks, sources, *refs):
    rows, pieces, (out_ref, held) = refs[:blocks], refs[blocks:-2], refs[-2:]
    depth = rows[0].shape[1] // sources.shape[0]
    start = 0
    for block in rows:
        stop = start + block.shape[0]
        for k in range(sources.shape[0]):
            columns = pl.ds(pl.multiple_of(sources[k] * depth, depth), depth)
            held[start:stop, k * depth : (k + 1) * depth] = block[:, columns]
        start = stop
    width = out_ref.shape[1]
    tile = width // 2
    for at in range(0, width, tile):
        gate = up = 0.0
        first = 0
        for piece in pieces:
            last = first + piece.shape[0]
            acts = held[:, first:last]
            gate += jnp.dot(acts, piece[:, at : at + tile], preferred_element_type=F32)
            up += jnp.dot(
                acts, piece[:, width + at : width + at + tile], preferred_element_type=F32
            )
            first = last
        out_ref[:, at : at + tile] = (gate / (1.0 + jnp.exp(-gate)) * up).astype(BF16)


def gate_up(blocks, pieces, sources):
    count = sum(block.shape[0] for block in blocks)
    depth = blocks[0].shape[1]
    width = pieces[0].shape[1]
    vmem = pl.BlockSpec(memory_space=pltpu.VMEM)
    return pl.pallas_call(
        functools.partial(gate_kernel, len(blocks)),
        in_specs=[pl.BlockSpec(memory_space=pltpu.SMEM)] + [vmem] * (len(blocks) + len(pieces)),
        out_specs=vmem,
        out_shape=jax.ShapeDtypeStruct((count, width // 2), BF16),
        scratch_shapes=[pltpu.VMEM((count, depth), BF16)],
        compiler_params=pltpu.CompilerParams(vmem_limit_bytes=40 * 1024 * 1024),
        cost_estimate=pl.CostEstimate(
            flops=2 * count * depth * width,
            bytes_accessed=2 * (count * depth + depth * width),
            transcendentals=count * width // 2,
        ),
        name="gate_up",
    )(sources, *blocks, *pieces)


def down_kernel(acts_ref, *refs):
    pieces, halves = refs[:-2], refs[-2:]
    depth = acts_ref.shape[1]
    width = pieces[0].shape[1]
    slices = [(piece, at) for piece in pieces for at in range(0, piece.shape[0], depth)]
    for k, (piece, at) in enumerate(slices):
        place = k % 2 * width
        halves[k // 2][:, place : place + width] = jnp.dot(
            acts_ref[...], piece[at : at + depth, :], preferred_element_type=F32
        ).astype(BF16)


def down(acts, pieces):
    rows, depth = acts.shape
    width = pieces[0].shape[1] * sum(piece.shape[0] for piece in pieces) // depth // 2
    vmem = pl.BlockSpec(memory_space=pltpu.VMEM)
    return pl.pallas_call(
        down_kernel,
        in_specs=[vmem] * (1 + len(pieces)),
        out_specs=[vmem, vmem],
        out_shape=[jax.ShapeDtypeStruct((rows, width), BF16)] * 2,
        compiler_params=pltpu.CompilerParams(vmem_limit_bytes=40 * 1024 * 1024),
        cost_estimate=pl.CostEstimate(
            flops=4 * rows * depth * width,
            bytes_accessed=4 * (rows + depth) * width,
            transcendentals=0,
        ),
        name="down",
    )(acts, *pieces)


def finish_kernel(sources, pair_sources, mixed_ref, own_ref, pair_ref, out_ref, total):
    count = sources.shape[0]
    width = mixed_ref.shape[1] // count

    def at(place):
        return pl.ds(pl.multiple_of(place * width, width), width)

    for k in range(count):
        columns = at(sources[k])
        total[:, columns] = mixed_ref[:, columns] + own_ref[:, k * width : (k + 1) * width]
    for k in range(count):
        columns = at(pair_sources[k])
        pair = pair_ref[:, k * width : (k + 1) * width].astype(F32)
        out_ref[:, columns] = (total[:, columns] + pair).astype(BF16)


def finish(mixed, own, pair, sources, pair_sources):
    vmem = pl.BlockSpec(memory_space=pltpu.VMEM)
    smem = pl.BlockSpec(memory_space=pltpu.SMEM)
    return pl.pallas_call(
        finish_kernel,
        in_specs=[smem, smem, vmem, vmem, vmem],
        out_specs=vmem,
        out_shape=jax.ShapeDtypeStruct(mixed.shape, BF16),
        scratch_shapes=[pltpu.VMEM(mixed.shape, F32)],
        compiler_params=pltpu.CompilerParams(vmem_limit_bytes=16 * 1024 * 1024),
        name="finish",
    )(sources, pair_sources, mixed, own, pair)


def body(
    hidden,
    request_of,
    positions,
    page_table,
    attn_gain,
    mlp_gain,
    wq,
    wk,
    wv,
    wo,
    w_gate,
    w_up,
    w_down,
):
    groups = lax.axis_size("group")
    me = lax.axis_index("tensor")
    group = lax.axis_index("group")
    odd = group % 2 == 1
    tok_group = request_of.shape[0]
    depth = hidden.shape[1]
    rows_dev = hidden.shape[0]
    def order_of(plane):
        alike = [plane % 2 + k for k in range(0, groups, 2)]
        return jnp.stack(alike + [(plane - k) % groups for k in (1, 3)]).astype(jnp.int32)

    sources, pair_sources = order_of(group), order_of(group ^ 1)
    starts = []
    for k in ORDER:
        first = (me ^ k) * rows_dev
        starts += [first, first + rows_dev // 2] if k in (6, 7) else [first]
    places = jnp.stack(starts).astype(jnp.int32)

    small = jnp.concatenate([wq.astype(BF16), wk.astype(BF16), wv.astype(BF16)], axis=1)
    qkv_weight = lax.all_gather(small, "group", axis=0, tiled=True)
    own_normed = rms_scale(hidden.astype(F32), attn_gain)
    firsts = gather_first(own_normed)
    ff = w_gate.shape[1] // 2
    gate_b, up_b, down_b = w_gate.astype(BF16), w_up.astype(BF16), w_down.astype(BF16)
    lower = jnp.concatenate([gate_b[:, :ff], up_b[:, :ff]], axis=1)
    upper = jnp.concatenate([gate_b[:, ff:], up_b[:, ff:]], axis=1)
    mine_in = jnp.where(odd, upper, lower)
    other_in = jnp.where(odd, lower, upper)
    mine_out = jnp.where(odd, down_b[ff:], down_b[:ff])
    other_out = jnp.where(odd, down_b[:ff], down_b[ff:])
    firsts, mine_in, other_in, mine_out, other_out = tied(
        firsts, mine_in, other_in, mine_out, other_out
    )
    far = gather_far(firsts)
    near = near_blocks(own_normed, firsts, far)
    normed = near + over(near)
    out_weight = lax.all_gather(wo.astype(BF16), "group", axis=1, tiled=True)

    half_dim = HD // 2
    frequency = rope_base ** (-(jnp.arange(half_dim, dtype=F32) * 2.0 / HD))
    angle = positions.astype(F32)[:, None] * frequency[None, :]
    cosine, sine = jnp.cos(angle), jnp.sin(angle)
    cosine = jnp.concatenate([cosine, cosine], axis=1)
    sine = jnp.concatenate([-sine, sine], axis=1)

    queries, kv_rows = project(normed, qkv_weight, cosine, sine, places)
    earlier = from_behind(kv_rows[-REACH:])
    places_in = positions[:, None]
    late = attend(queries, kv_rows, places_in, REACH, tok_group)
    early_kv = jnp.concatenate([earlier, kv_rows[:REACH]], axis=0)
    early = attend(queries, early_kv, places_in, 0, REACH)
    attended = jnp.concatenate([early, late], axis=0)

    started = positions[0] >= 0

    alike_in = gather_alternate(after(mine_in, kv_rows))
    alike_out = gather_alternate(after(mine_out, kv_rows))

    pages = page_table.shape[1]
    changed = jnp.concatenate(
        [jnp.ones((1,), jnp.int32), (request_of[1:] != request_of[:-1]).astype(jnp.int32)]
    )
    opens = jnp.maximum(changed, (positions % PAGE == 0).astype(jnp.int32))
    logical = jnp.cumsum(opens) - 1
    chosen = jnp.sum(
        jnp.where(logical[:, None] == jnp.arange(pages)[None, :], page_table, 0), axis=1
    )
    target = chosen * PAGE + positions % PAGE
    width = kv_rows.shape[1]

    four = len(ORDER) // 2
    block_places = jnp.stack([(me ^ k) * rows_dev for k in ORDER]).astype(jnp.int32)

    def to_blocks(attended, out_weight, block_places, hidden, gain, other_in, target, kv_rows):
        other = mix(attended, out_weight, block_places[four:], rows_dev)
        mine = mix(attended, out_weight, block_places[:four], rows_dev)
        mixed = hidden.astype(F32) + scatter_last(scatter_first(mine, other))
        own_rows = rms_scale(mixed, gain)
        pair_rows = pair_swap(own_rows)
        firsts = gather_first(own_rows)
        cache = jnp.zeros((pages * PAGE, kv_rows.shape[1]), BF16).at[target].set(kv_rows)
        firsts, cache = tied(firsts, cache)
        own_near = near_blocks(own_rows, firsts, gather_far(firsts))
        own_blocks = [own_near, over(own_near)]
        near_in = turn(after(other_in, own_near), 1)
        firsts = gather_first(after(pair_rows, own_near))
        firsts, near_in = tied(firsts, near_in)
        far_in = turn(after(other_in, pair_rows), 3)
        pair_near = near_blocks(pair_rows, firsts, gather_far(firsts))
        return mixed, own_blocks, [pair_near, over(pair_near)], near_in, far_in, cache

    mixed, own_blocks, other_blocks, near_in, far_in, cache = step(
        started,
        to_blocks,
        attended,
        out_weight,
        block_places,
        hidden,
        mlp_gain,
        other_in,
        target,
        kv_rows,
    )
    in_pieces = [alike_in, near_in, far_in]
    own_blocks, alike_out = tied(own_blocks, alike_out)
    other_out = after(other_out, far_in)
    out_pieces = [alike_out, turn(other_out, 1), turn(other_out, 3)]

    def acts_of(blocks):
        near, across = blocks
        return gate_up(across, in_pieces, sources), gate_up(near, in_pieces, sources)

    own_acts = acts_of(own_blocks)
    other_acts = acts_of(other_blocks)
    other_acts, out_pieces[1:] = tied(other_acts, out_pieces[1:])

    other, mine = (down(half, out_pieces) for half in other_acts)
    pair_parts = scatter_first(mine, other)
    other, mine = (down(half, out_pieces) for half in own_acts)
    other, mine = after((other, mine), pair_parts)
    own_parts = scatter_first(mine, other)
    pair_sum = scatter_last(pair_parts).astype(BF16)
    from_pair = pair_swap(pair_sum)
    own_parts = after(own_parts, from_pair)
    own_sum = scatter_last(own_parts)
    layer_out = finish(mixed, own_sum, from_pair, sources, pair_sources)
    return (layer_out, cache.reshape(pages, PAGE, width))


def partner(value, axis, distance):
    mask = 2**distance
    pairs = [(source, source ^ mask) for source in range(lax.axis_size(axis))]
    return lax.ppermute(value, axis, pairs)


def plain_from_behind(block, axis, distance):
    devices = range(lax.axis_size(axis))
    route = [(i - distance, i) for i in devices if i - distance in devices]
    return lax.ppermute(block, axis, route)


def plain_rms_scale(values, gain):
    square = jnp.mean(values * values, axis=-1, keepdims=True)
    return (values * lax.rsqrt(square + norm_eps) * gain).astype(jnp.bfloat16)


def rotate(values, places):
    half_dim = values.shape[-1] // 2
    frequency = rope_base ** (-(jnp.arange(half_dim, dtype=jnp.float32) * 2.0 / values.shape[-1]))
    angle = places.astype(jnp.float32)[:, None] * frequency[None, :]
    cosine = jnp.cos(angle)[:, None, :]
    sine = jnp.sin(angle)[:, None, :]
    widened = values.astype(jnp.float32)
    first = widened[..., :half_dim]
    second = widened[..., half_dim:]
    return jnp.concatenate(
        [first * cosine - second * sine, second * cosine + first * sine], axis=-1
    ).astype(jnp.bfloat16)


def join_halves(own_part, other_part):
    even = lax.axis_index("tensor") % 2 == 0
    lower = jnp.where(even, own_part, other_part)
    upper = jnp.where(even, other_part, own_part)
    return jnp.concatenate([lower, upper], axis=-1)


def contract_rows(acts, pieces):
    return tuple((jnp.dot(acts, piece, preferred_element_type=jnp.float32) for piece in pieces))


def plain_body(
    hidden,
    request_of,
    positions,
    page_table,
    attn_gain,
    mlp_gain,
    wq,
    wk,
    wv,
    wo,
    w_gate,
    w_up,
    w_down,
):
    tensor_count = lax.axis_size("tensor")
    rows_dev = hidden.shape[0]
    tok_group = request_of.shape[0]
    query_heads = QH // tensor_count
    key_heads = max(1, KVH // tensor_count)
    group_ratio = QH // KVH
    paired = tensor_count > KVH
    residual = lax.all_gather(hidden, "tensor", axis=0, tiled=True).astype(jnp.float32)
    normed = plain_rms_scale(residual, attn_gain)
    query_rows = wq.astype(jnp.bfloat16)
    key_rows = wk.astype(jnp.bfloat16)
    value_rows = wv.astype(jnp.bfloat16)
    if paired:
        other_key, other_value = partner((key_rows, value_rows), "tensor", 0)
        key_rows = join_halves(key_rows, other_key)
        value_rows = join_halves(value_rows, other_value)
    query_sum, key_sum, value_sum = contract_rows(
        normed,
        (
            lax.all_gather(query_rows, "group", axis=0, tiled=True),
            lax.all_gather(key_rows, "group", axis=0, tiled=True),
            lax.all_gather(value_rows, "group", axis=0, tiled=True),
        ),
    )
    query_raw = query_sum.astype(jnp.bfloat16)
    key_raw = key_sum.astype(jnp.bfloat16)
    value_raw = value_sum.astype(jnp.bfloat16)
    queries = rotate(query_raw.reshape(tok_group, query_heads, HD), positions)
    keys = rotate(key_raw.reshape(tok_group, key_heads, HD), positions)
    values = value_raw.reshape(tok_group, key_heads, HD)
    kv_rows = jnp.stack([keys, values], axis=2)
    earlier = plain_from_behind(kv_rows, "group", 1)
    earlier_rows = earlier.shape[0]
    all_rows = jnp.concatenate([earlier, kv_rows], axis=0)
    all_keys = jnp.repeat(all_rows[:, :, 0], group_ratio, axis=1)[:, :query_heads]
    all_values = jnp.repeat(all_rows[:, :, 1], group_ratio, axis=1)[:, :query_heads]
    first_request = request_of[0]
    first_position = positions[0]
    same_local = (request_of[:, None] == request_of[None, :]) & (
        positions[None, :] <= positions[:, None]
    )
    same_earlier = (request_of[:, None] == first_request) & (
        jnp.arange(earlier_rows)[None, :] >= earlier_rows - first_position
    )
    visible = jnp.concatenate([same_earlier, same_local], axis=1)
    scores = jnp.einsum(
        "qhd,khd->hqk", queries, all_keys, preferred_element_type=jnp.float32
    ) * HD ** (-0.5)
    scores = jnp.where(visible[None], scores, -1e30)
    row_peak = jnp.max(scores, axis=-1, keepdims=True)
    probs = jnp.where(visible[None], jnp.exp(scores - row_peak), 0.0)
    total = jnp.sum(probs, axis=-1, keepdims=True)
    mixed_heads = jnp.einsum(
        "hqk,khd->qhd", probs.astype(jnp.bfloat16), all_values, preferred_element_type=jnp.float32
    ) / jnp.transpose(total, (1, 0, 2))
    attended = mixed_heads.astype(jnp.bfloat16).reshape(tok_group, query_heads * HD)
    out_rows = wo.astype(jnp.bfloat16)
    attn_part = jnp.dot(
        attended,
        lax.all_gather(out_rows, "group", axis=1, tiled=True),
        preferred_element_type=jnp.float32,
    )
    mixed = residual + lax.psum(attn_part.astype(jnp.bfloat16), "tensor").astype(jnp.float32)
    normed_mlp = plain_rms_scale(mixed, mlp_gain)
    gate_rows = w_gate.astype(jnp.bfloat16)
    up_rows = w_up.astype(jnp.bfloat16)
    gate_sum, up_sum = contract_rows(
        normed_mlp,
        (
            lax.all_gather(gate_rows, "group", axis=0, tiled=True),
            lax.all_gather(up_rows, "group", axis=0, tiled=True),
        ),
    )
    activation = (jax.nn.silu(gate_sum) * up_sum).astype(jnp.bfloat16)
    down_rows = w_down.astype(jnp.bfloat16)
    down_part = jnp.dot(
        activation,
        lax.all_gather(down_rows, "group", axis=1, tiled=True),
        preferred_element_type=jnp.float32,
    )
    summed = lax.psum(down_part.astype(jnp.bfloat16), "tensor").astype(jnp.float32)
    first_row = lax.axis_index("tensor") * rows_dev
    own_mixed = lax.dynamic_slice_in_dim(mixed, first_row, rows_dev, 0)
    own_summed = lax.dynamic_slice_in_dim(summed, first_row, rows_dev, 0)
    layer_out = (own_mixed + own_summed).astype(jnp.bfloat16)
    pages = page_table.shape[1]
    changed = jnp.concatenate(
        [jnp.ones((1,), jnp.int32), (request_of[1:] != request_of[:-1]).astype(jnp.int32)]
    )
    opens = jnp.maximum(changed, (positions % PAGE == 0).astype(jnp.int32))
    logical = jnp.cumsum(opens) - 1
    chosen = jnp.sum(
        jnp.where(logical[:, None] == jnp.arange(pages)[None, :], page_table, 0), axis=1
    )
    target = chosen * PAGE + positions % PAGE
    width = 2 * KVH * HD // tensor_count
    flat_rows = kv_rows.reshape(tok_group, key_heads * 2 * HD)
    offset = lax.axis_index("tensor") * width % (key_heads * 2 * HD)
    own_slice = lax.dynamic_slice_in_dim(flat_rows, offset, width, 1)
    cache = jnp.zeros((pages * PAGE, width), jnp.bfloat16).at[target].set(own_slice)
    return (layer_out, cache.reshape(pages, PAGE, width))


def solution(mesh):
    shaped = mesh.shape["tensor"] == len(ORDER) and mesh.shape["group"] == 4
    placed = (
        P(("group", "tensor"), None),
        P("group"),
        P("group"),
        P("group", None),
        P(),
        P(),
        P("group", "tensor"),
        P("group", "tensor"),
        P("group", "tensor"),
        P("tensor", "group"),
        P("group", "tensor"),
        P("group", "tensor"),
        P("tensor", "group"),
    )
    return jax.shard_map(
        body if shaped else plain_body,
        mesh=mesh,
        in_specs=placed,
        out_specs=(P(("group", "tensor"), None), P("group", None, "tensor")),
        check_vma=False,
    )
```

```python
import functools

import jax
import jax.numpy as jnp
from jax import lax
from jax.experimental import pallas as pl
from jax.experimental.pallas import tpu as pltpu
from jax.sharding import PartitionSpec as P

QH = 16
KVH = 8
HD = 128
PAGE = 128
REACH = 512

rope_base = 1000000.0
norm_eps = 1e-06

F32 = jnp.float32
BF16 = jnp.bfloat16

ORDER = (2, 6, 4, 0, 3, 7, 5, 1)


def swap(value, distance):
    return lax.ppermute(
        value, "tensor", [(i, i ^ distance) for i in range(lax.axis_size("tensor"))]
    )


def turn(value, distance):
    count = lax.axis_size("group")
    return lax.ppermute(value, "group", [(i, (i + distance) % count) for i in range(count)])


def pair_swap(value):
    return lax.ppermute(value, "group", [(i, i ^ 1) for i in range(lax.axis_size("group"))])


def gather_alternate(value):
    count = lax.axis_size("group")
    return lax.all_gather(
        value,
        "group",
        axis=0,
        tiled=True,
        axis_index_groups=[list(range(m, count, 2)) for m in range(2)],
    )


def from_behind(block):
    count = lax.axis_size("group")
    return lax.ppermute(block, "group", [(i, i + 1) for i in range(count - 1)])


def tied(*values):
    return lax.optimization_barrier(values)


def step(started, function, *operands):
    shapes = jax.eval_shape(function, *operands)

    def nothing(*operands):
        return jax.tree.map(lambda leaf: jnp.zeros(leaf.shape, leaf.dtype), shapes)

    return lax.cond(started, function, nothing, *operands)


def after(value, *others):
    return lax.optimization_barrier((value, *others))[0]


def rms_scale(values, gain):
    square = jnp.mean(values * values, axis=-1, keepdims=True)
    return (values * lax.rsqrt(square + norm_eps) * gain).astype(BF16)


def gather_first(own):
    return swap(own, 2), swap(own, 4)


def gather_far(firsts):
    by_x, by_y = firsts
    half = by_x.shape[0] // 2
    return swap(by_x[:half], 4), swap(by_y[half:], 2)


def near_blocks(own, firsts, far):
    return [firsts[0], far[0], far[1], firsts[1], own]


def over(near):
    return [swap(block, 1) for block in near]


def wide_sum(*terms):
    total = terms[0].astype(F32)
    for term in terms[1:]:
        total = total + term.astype(F32)
    return total


def scatter_first(mine, other):
    got_left, got_right = (swap(half, 1) for half in other)
    left, right = mine
    rows = left.shape[0] // 4
    left_in = swap(wide_sum(left[: 2 * rows], got_left[: 2 * rows]).astype(BF16), 2)
    right_in = swap(wide_sum(right[rows : 3 * rows], got_right[rows : 3 * rows]).astype(BF16), 4)
    return left, right, got_left, got_right, left_in, right_in


def scatter_last(parts):
    left, right, got_left, got_right, left_in, right_in = parts
    rows = left.shape[0] // 4
    two, three = 2 * rows, 3 * rows
    left_on = wide_sum(left[two:three], got_left[two:three], left_in[rows:]).astype(BF16)
    right_on = wide_sum(right[:rows], got_right[:rows], right_in[:rows]).astype(BF16)
    left_last = swap(left_on, 4)
    right_last = swap(right_on, 2)
    return jnp.concatenate(
        [
            wide_sum(left[three:], got_left[three:], left_in[:rows], left_last),
            wide_sum(right[three:], got_right[three:], right_in[rows:], right_last),
        ],
        axis=1,
    )


def pack_kernel(*refs):
    out_ref = refs[-1]
    at = 0
    for ref in refs[:-1]:
        width = ref.shape[1]
        out_ref[:, at : at + width] = ref[...].astype(BF16)
        at += width


def pack(*weights):
    vmem = pl.BlockSpec(memory_space=pltpu.VMEM)
    width = sum(weight.shape[1] for weight in weights)
    return pl.pallas_call(
        pack_kernel,
        in_specs=[vmem] * len(weights),
        out_specs=vmem,
        out_shape=jax.ShapeDtypeStruct((weights[0].shape[0], width), BF16),
        name="pack",
    )(*weights)


def project_kernel(blocks, places, *refs):
    rows, (w_ref, cos_ref, sin_ref, q_ref, kv_ref) = refs[:blocks], refs[blocks:]
    heads = q_ref.shape[1] // HD
    for b, block in enumerate(rows):
        size = block.shape[0]
        raw = jnp.dot(block[...], w_ref[...], preferred_element_type=F32).astype(BF16)
        here = pl.ds(pl.multiple_of(places[b], 32), size)
        cosine = cos_ref[here, :]
        sine = sin_ref[here, :]

        def rotated(head):
            wide = raw[:, head * HD : (head + 1) * HD].astype(F32)
            turned = jnp.concatenate([wide[:, HD // 2 :], wide[:, : HD // 2]], axis=1)
            return (wide * cosine + turned * sine).astype(BF16)

        for head in range(heads):
            q_ref[here, head * HD : (head + 1) * HD] = rotated(head)
        kv_ref[here, :HD] = rotated(heads)
        kv_ref[here, HD:] = raw[:, (heads + 1) * HD :]


def project(blocks, weight, cosine, sine, places):
    rows = cosine.shape[0]
    depth, width = weight.shape
    vmem = pl.BlockSpec(memory_space=pltpu.VMEM)
    smem = pl.BlockSpec(memory_space=pltpu.SMEM)
    return pl.pallas_call(
        functools.partial(project_kernel, len(blocks)),
        in_specs=[smem] + [vmem] * (len(blocks) + 3),
        out_specs=[vmem, vmem],
        out_shape=[
            jax.ShapeDtypeStruct((rows, width - 2 * HD), BF16),
            jax.ShapeDtypeStruct((rows, 2 * HD), BF16),
        ],
        compiler_params=pltpu.CompilerParams(vmem_limit_bytes=40 * 1024 * 1024),
        cost_estimate=pl.CostEstimate(
            flops=2 * rows * depth * width,
            bytes_accessed=2 * (rows * depth + depth * width),
            transcendentals=0,
        ),
        name="project",
    )(places, *blocks, weight, cosine, sine)


def attend_kernel(q_ref, kv_ref, pos_ref, out_ref):
    step = pl.program_id(0)
    size = q_ref.shape[0]
    span = size + REACH
    window = pl.ds(pl.multiple_of(step * size, size), span)
    keys = kv_ref[window, :HD]
    values = kv_ref[window, HD:]
    row = lax.broadcasted_iota(jnp.int32, (size, span), 0)
    column = lax.broadcasted_iota(jnp.int32, (size, span), 1)
    back = row + REACH - column
    visible = (back >= 0) & (back <= pos_ref[...])
    for head in range(q_ref.shape[1] // HD):
        query = q_ref[:, head * HD : (head + 1) * HD]
        scores = lax.dot_general(
            query, keys, (((1,), (1,)), ((), ())), preferred_element_type=F32
        ) * HD ** (-0.5)
        scores = jnp.where(visible, scores, -1e30)
        peak = jnp.max(scores, axis=1, keepdims=True)
        probs = jnp.exp(scores - peak)
        total = jnp.sum(probs, axis=1, keepdims=True)
        mixed = jnp.dot(probs.astype(BF16), values, preferred_element_type=F32)
        out_ref[:, head * HD : (head + 1) * HD] = (mixed / total).astype(BF16)


def attend(queries, keys_values, positions, first, last):
    size = 256
    width = queries.shape[1]
    rows = last - first
    skip = first // size
    return pl.pallas_call(
        attend_kernel,
        grid=(rows // size,),
        in_specs=[
            pl.BlockSpec((size, width), lambda i: (i + skip, 0)),
            pl.BlockSpec(keys_values.shape, lambda i: (0, 0)),
            pl.BlockSpec((size, 1), lambda i: (i + skip, 0)),
        ],
        out_specs=pl.BlockSpec((size, width), lambda i: (i, 0)),
        out_shape=jax.ShapeDtypeStruct((rows, width), BF16),
        compiler_params=pltpu.CompilerParams(vmem_limit_bytes=32 * 1024 * 1024),
        cost_estimate=pl.CostEstimate(
            flops=4 * rows * (size + REACH) * width,
            bytes_accessed=4 * rows * width,
            transcendentals=rows * (size + REACH) * width // HD,
        ),
        name="attend",
    )(queries, keys_values, positions)


def mix_kernel(rows, places, x_ref, w_ref, left_ref, right_ref):
    depth = x_ref.shape[1]
    width = w_ref.shape[1]
    for b in range(places.shape[0]):
        block = x_ref[pl.ds(pl.multiple_of(places[b], 32), rows), :]
        for k in range(w_ref.shape[0] // depth):
            half = (left_ref, right_ref)[k // 2]
            at = k % 2 * width
            half[b * rows : (b + 1) * rows, at : at + width] = jnp.dot(
                block, w_ref[k * depth : (k + 1) * depth, :], preferred_element_type=F32
            ).astype(BF16)


def mix(attended, weight, places, rows):
    count = places.shape[0] * rows
    depth = attended.shape[1]
    width = weight.size // depth
    vmem = pl.BlockSpec(memory_space=pltpu.VMEM)
    return pl.pallas_call(
        functools.partial(mix_kernel, rows),
        in_specs=[pl.BlockSpec(memory_space=pltpu.SMEM), vmem, vmem],
        out_specs=[vmem, vmem],
        out_shape=[jax.ShapeDtypeStruct((count, width // 2), BF16)] * 2,
        compiler_params=pltpu.CompilerParams(vmem_limit_bytes=40 * 1024 * 1024),
        cost_estimate=pl.CostEstimate(
            flops=2 * count * depth * width,
            bytes_accessed=2 * count * width,
            transcendentals=0,
        ),
        name="mix",
    )(places, attended, weight)


def gate_kernel(blocks, sources, *refs):
    rows, pieces, (out_ref, held) = refs[:blocks], refs[blocks:-2], refs[-2:]
    depth = rows[0].shape[1] // sources.shape[0]
    start = 0
    for block in rows:
        stop = start + block.shape[0]
        for k in range(sources.shape[0]):
            columns = pl.ds(pl.multiple_of(sources[k] * depth, depth), depth)
            held[start:stop, k * depth : (k + 1) * depth] = block[:, columns]
        start = stop
    width = out_ref.shape[1]
    tile = width // 2
    for at in range(0, width, tile):
        gate = up = 0.0
        first = 0
        for piece in pieces:
            last = first + piece.shape[0]
            acts = held[:, first:last]
            gate += jnp.dot(acts, piece[:, at : at + tile], preferred_element_type=F32)
            up += jnp.dot(
                acts, piece[:, width + at : width + at + tile], preferred_element_type=F32
            )
            first = last
        out_ref[:, at : at + tile] = (gate / (1.0 + jnp.exp(-gate)) * up).astype(BF16)


def gate_up(blocks, pieces, sources):
    count = sum(block.shape[0] for block in blocks)
    depth = blocks[0].shape[1]
    width = pieces[0].shape[1]
    vmem = pl.BlockSpec(memory_space=pltpu.VMEM)
    return pl.pallas_call(
        functools.partial(gate_kernel, len(blocks)),
        in_specs=[pl.BlockSpec(memory_space=pltpu.SMEM)] + [vmem] * (len(blocks) + len(pieces)),
        out_specs=vmem,
        out_shape=jax.ShapeDtypeStruct((count, width // 2), BF16),
        scratch_shapes=[pltpu.VMEM((count, depth), BF16)],
        compiler_params=pltpu.CompilerParams(vmem_limit_bytes=40 * 1024 * 1024),
        cost_estimate=pl.CostEstimate(
            flops=2 * count * depth * width,
            bytes_accessed=2 * (count * depth + depth * width),
            transcendentals=count * width // 2,
        ),
        name="gate_up",
    )(sources, *blocks, *pieces)


def down_kernel(acts_ref, *refs):
    pieces, out_ref = refs[:-1], refs[-1]
    depth = acts_ref.shape[1]
    width = pieces[0].shape[1]
    slices = [(piece, at) for piece in pieces for at in range(0, piece.shape[0], depth)]
    for k, (piece, at) in enumerate(slices):
        out_ref[:, k * width : (k + 1) * width] = jnp.dot(
            acts_ref[...], piece[at : at + depth, :], preferred_element_type=F32
        ).astype(BF16)


def down(acts, pieces):
    rows, depth = acts.shape
    width = sum(piece.size for piece in pieces) // depth
    vmem = pl.BlockSpec(memory_space=pltpu.VMEM)
    return pl.pallas_call(
        down_kernel,
        in_specs=[vmem] * (1 + len(pieces)),
        out_specs=vmem,
        out_shape=jax.ShapeDtypeStruct((rows, width), BF16),
        compiler_params=pltpu.CompilerParams(vmem_limit_bytes=40 * 1024 * 1024),
        cost_estimate=pl.CostEstimate(
            flops=2 * rows * depth * width,
            bytes_accessed=2 * (rows + depth) * width,
            transcendentals=0,
        ),
        name="down",
    )(acts, *pieces)


def finish_kernel(sources, pair_sources, mixed_ref, own_ref, pair_ref, out_ref, total):
    count = sources.shape[0]
    width = mixed_ref.shape[1] // count

    def at(place):
        return pl.ds(pl.multiple_of(place * width, width), width)

    for k in range(count):
        columns = at(sources[k])
        total[:, columns] = mixed_ref[:, columns] + own_ref[:, k * width : (k + 1) * width]
    for k in range(count):
        columns = at(pair_sources[k])
        pair = pair_ref[:, k * width : (k + 1) * width].astype(F32)
        out_ref[:, columns] = (total[:, columns] + pair).astype(BF16)


def finish(mixed, own, pair, sources, pair_sources):
    vmem = pl.BlockSpec(memory_space=pltpu.VMEM)
    smem = pl.BlockSpec(memory_space=pltpu.SMEM)
    return pl.pallas_call(
        finish_kernel,
        in_specs=[smem, smem, vmem, vmem, vmem],
        out_specs=vmem,
        out_shape=jax.ShapeDtypeStruct(mixed.shape, BF16),
        scratch_shapes=[pltpu.VMEM(mixed.shape, F32)],
        compiler_params=pltpu.CompilerParams(vmem_limit_bytes=16 * 1024 * 1024),
        name="finish",
    )(sources, pair_sources, mixed, own, pair)


def body(
    hidden,
    request_of,
    positions,
    page_table,
    attn_gain,
    mlp_gain,
    wq,
    wk,
    wv,
    wo,
    w_gate,
    w_up,
    w_down,
):
    groups = lax.axis_size("group")
    me = lax.axis_index("tensor")
    group = lax.axis_index("group")
    odd = group % 2 == 1
    tok_group = request_of.shape[0]
    depth = hidden.shape[1]
    rows_dev = hidden.shape[0]
    def order_of(plane):
        alike = [plane % 2 + k for k in range(0, groups, 2)]
        return jnp.stack(alike + [(plane - k) % groups for k in (1, 3)]).astype(jnp.int32)

    sources, pair_sources = order_of(group), order_of(group ^ 1)
    starts = []
    for k in ORDER:
        first = (me ^ k) * rows_dev
        starts += [first, first + rows_dev // 2] if k in (6, 7) else [first]
    places = jnp.stack(starts).astype(jnp.int32)

    small = pack(wq, wk, wv)
    qkv_weight = lax.all_gather(small, "group", axis=0, tiled=True)
    own_normed = rms_scale(hidden.astype(F32), attn_gain)
    firsts = gather_first(own_normed)
    ff = w_gate.shape[1] // 2
    gate_b, up_b, down_b = w_gate.astype(BF16), w_up.astype(BF16), w_down.astype(BF16)
    lower = jnp.concatenate([gate_b[:, :ff], up_b[:, :ff]], axis=1)
    upper = jnp.concatenate([gate_b[:, ff:], up_b[:, ff:]], axis=1)
    mine_in = jnp.where(odd, upper, lower)
    other_in = jnp.where(odd, lower, upper)
    mine_out = jnp.where(odd, down_b[ff:], down_b[:ff])
    other_out = jnp.where(odd, down_b[:ff], down_b[ff:])
    firsts, mine_in, other_in, mine_out, other_out = tied(
        firsts, mine_in, other_in, mine_out, other_out
    )
    far = gather_far(firsts)
    near = near_blocks(own_normed, firsts, far)
    normed = near + over(near)
    out_weight = lax.all_gather(wo.astype(BF16), "group", axis=0, tiled=True)

    half_dim = HD // 2
    frequency = rope_base ** (-(jnp.arange(half_dim, dtype=F32) * 2.0 / HD))
    angle = positions.astype(F32)[:, None] * frequency[None, :]
    cosine, sine = jnp.cos(angle), jnp.sin(angle)
    cosine = jnp.concatenate([cosine, cosine], axis=1)
    sine = jnp.concatenate([-sine, sine], axis=1)

    queries, kv_rows = project(normed, qkv_weight, cosine, sine, places)
    earlier = from_behind(kv_rows[-REACH:])
    places_in = positions[:, None]
    late = attend(queries, kv_rows, places_in, REACH, tok_group)
    early_kv = jnp.concatenate([earlier, kv_rows[:REACH]], axis=0)
    early = attend(queries, early_kv, places_in, 0, REACH)
    attended = jnp.concatenate([early, late], axis=0)

    started = positions[0] >= 0

    alike_in = gather_alternate(after(mine_in, kv_rows))
    alike_out = gather_alternate(after(mine_out, kv_rows))

    pages = page_table.shape[1]
    changed = jnp.concatenate(
        [jnp.ones((1,), jnp.int32), (request_of[1:] != request_of[:-1]).astype(jnp.int32)]
    )
    opens = jnp.maximum(changed, (positions % PAGE == 0).astype(jnp.int32))
    logical = jnp.cumsum(opens) - 1
    chosen = jnp.sum(
        jnp.where(logical[:, None] == jnp.arange(pages)[None, :], page_table, 0), axis=1
    )
    target = chosen * PAGE + positions % PAGE
    width = kv_rows.shape[1]

    four = len(ORDER) // 2
    block_places = jnp.stack([(me ^ k) * rows_dev for k in ORDER]).astype(jnp.int32)

    def to_blocks(attended, out_weight, block_places, hidden, gain, other_in, target, kv_rows):
        other = mix(attended, out_weight, block_places[four:], rows_dev)
        mine = mix(attended, out_weight, block_places[:four], rows_dev)
        mixed = hidden.astype(F32) + scatter_last(scatter_first(mine, other))
        own_rows = rms_scale(mixed, gain)
        pair_rows = pair_swap(own_rows)
        firsts = gather_first(own_rows)
        cache = jnp.zeros((pages * PAGE, kv_rows.shape[1]), BF16).at[target].set(kv_rows)
        firsts, cache = tied(firsts, cache)
        own_near = near_blocks(own_rows, firsts, gather_far(firsts))
        own_blocks = [own_near, over(own_near)]
        near_in = turn(after(other_in, own_near), 1)
        firsts = gather_first(after(pair_rows, own_near))
        firsts, near_in = tied(firsts, near_in)
        far_in = turn(after(other_in, pair_rows), 3)
        pair_near = near_blocks(pair_rows, firsts, gather_far(firsts))
        return mixed, own_blocks, [pair_near, over(pair_near)], near_in, far_in, cache

    mixed, own_blocks, other_blocks, near_in, far_in, cache = step(
        started,
        to_blocks,
        attended,
        out_weight,
        block_places,
        hidden,
        mlp_gain,
        other_in,
        target,
        kv_rows,
    )
    in_pieces = [alike_in, near_in, far_in]
    own_blocks, alike_out = tied(own_blocks, alike_out)
    other_out = after(other_out, far_in)
    near_out, far_out = turn(other_out, 1), turn(other_out, 3)

    def acts_of(blocks):
        near, across = blocks
        return gate_up(across, in_pieces, sources), gate_up(near, in_pieces, sources)

    own_acts = acts_of(own_blocks)
    other_acts = acts_of(other_blocks)
    left = [down(half, [alike_out]) for half in other_acts]
    other_acts, out_pieces = tied(other_acts, [near_out, far_out])
    right = [down(half, out_pieces) for half in other_acts]
    pair_parts = scatter_first((left[1], right[1]), (left[0], right[0]))
    own_acts = after(own_acts, pair_parts)
    left = [down(half, [alike_out]) for half in own_acts]
    right = [down(half, out_pieces) for half in own_acts]
    mine, other = (left[1], right[1]), (left[0], right[0])
    own_parts = scatter_first(mine, other)
    pair_sum = scatter_last(pair_parts).astype(BF16)
    from_pair = pair_swap(pair_sum)
    own_parts = after(own_parts, from_pair)
    own_sum = scatter_last(own_parts)
    layer_out = finish(mixed, own_sum, from_pair, sources, pair_sources)
    return (layer_out, cache.reshape(pages, PAGE, width))


def partner(value, axis, distance):
    mask = 2**distance
    pairs = [(source, source ^ mask) for source in range(lax.axis_size(axis))]
    return lax.ppermute(value, axis, pairs)


def plain_from_behind(block, axis, distance):
    devices = range(lax.axis_size(axis))
    route = [(i - distance, i) for i in devices if i - distance in devices]
    return lax.ppermute(block, axis, route)


def plain_rms_scale(values, gain):
    square = jnp.mean(values * values, axis=-1, keepdims=True)
    return (values * lax.rsqrt(square + norm_eps) * gain).astype(jnp.bfloat16)


def rotate(values, places):
    half_dim = values.shape[-1] // 2
    frequency = rope_base ** (-(jnp.arange(half_dim, dtype=jnp.float32) * 2.0 / values.shape[-1]))
    angle = places.astype(jnp.float32)[:, None] * frequency[None, :]
    cosine = jnp.cos(angle)[:, None, :]
    sine = jnp.sin(angle)[:, None, :]
    widened = values.astype(jnp.float32)
    first = widened[..., :half_dim]
    second = widened[..., half_dim:]
    return jnp.concatenate(
        [first * cosine - second * sine, second * cosine + first * sine], axis=-1
    ).astype(jnp.bfloat16)


def join_halves(own_part, other_part):
    even = lax.axis_index("tensor") % 2 == 0
    lower = jnp.where(even, own_part, other_part)
    upper = jnp.where(even, other_part, own_part)
    return jnp.concatenate([lower, upper], axis=-1)


def contract_rows(acts, pieces):
    return tuple((jnp.dot(acts, piece, preferred_element_type=jnp.float32) for piece in pieces))


def plain_body(
    hidden,
    request_of,
    positions,
    page_table,
    attn_gain,
    mlp_gain,
    wq,
    wk,
    wv,
    wo,
    w_gate,
    w_up,
    w_down,
):
    tensor_count = lax.axis_size("tensor")
    rows_dev = hidden.shape[0]
    tok_group = request_of.shape[0]
    query_heads = QH // tensor_count
    key_heads = max(1, KVH // tensor_count)
    group_ratio = QH // KVH
    paired = tensor_count > KVH
    residual = lax.all_gather(hidden, "tensor", axis=0, tiled=True).astype(jnp.float32)
    normed = plain_rms_scale(residual, attn_gain)
    query_rows = wq.astype(jnp.bfloat16)
    key_rows = wk.astype(jnp.bfloat16)
    value_rows = wv.astype(jnp.bfloat16)
    if paired:
        other_key, other_value = partner((key_rows, value_rows), "tensor", 0)
        key_rows = join_halves(key_rows, other_key)
        value_rows = join_halves(value_rows, other_value)
    query_sum, key_sum, value_sum = contract_rows(
        normed,
        (
            lax.all_gather(query_rows, "group", axis=0, tiled=True),
            lax.all_gather(key_rows, "group", axis=0, tiled=True),
            lax.all_gather(value_rows, "group", axis=0, tiled=True),
        ),
    )
    query_raw = query_sum.astype(jnp.bfloat16)
    key_raw = key_sum.astype(jnp.bfloat16)
    value_raw = value_sum.astype(jnp.bfloat16)
    queries = rotate(query_raw.reshape(tok_group, query_heads, HD), positions)
    keys = rotate(key_raw.reshape(tok_group, key_heads, HD), positions)
    values = value_raw.reshape(tok_group, key_heads, HD)
    kv_rows = jnp.stack([keys, values], axis=2)
    earlier = plain_from_behind(kv_rows, "group", 1)
    earlier_rows = earlier.shape[0]
    all_rows = jnp.concatenate([earlier, kv_rows], axis=0)
    all_keys = jnp.repeat(all_rows[:, :, 0], group_ratio, axis=1)[:, :query_heads]
    all_values = jnp.repeat(all_rows[:, :, 1], group_ratio, axis=1)[:, :query_heads]
    first_request = request_of[0]
    first_position = positions[0]
    same_local = (request_of[:, None] == request_of[None, :]) & (
        positions[None, :] <= positions[:, None]
    )
    same_earlier = (request_of[:, None] == first_request) & (
        jnp.arange(earlier_rows)[None, :] >= earlier_rows - first_position
    )
    visible = jnp.concatenate([same_earlier, same_local], axis=1)
    scores = jnp.einsum(
        "qhd,khd->hqk", queries, all_keys, preferred_element_type=jnp.float32
    ) * HD ** (-0.5)
    scores = jnp.where(visible[None], scores, -1e30)
    row_peak = jnp.max(scores, axis=-1, keepdims=True)
    probs = jnp.where(visible[None], jnp.exp(scores - row_peak), 0.0)
    total = jnp.sum(probs, axis=-1, keepdims=True)
    mixed_heads = jnp.einsum(
        "hqk,khd->qhd", probs.astype(jnp.bfloat16), all_values, preferred_element_type=jnp.float32
    ) / jnp.transpose(total, (1, 0, 2))
    attended = mixed_heads.astype(jnp.bfloat16).reshape(tok_group, query_heads * HD)
    out_rows = wo.astype(jnp.bfloat16)
    attn_part = jnp.dot(
        attended,
        lax.all_gather(out_rows, "group", axis=1, tiled=True),
        preferred_element_type=jnp.float32,
    )
    mixed = residual + lax.psum(attn_part.astype(jnp.bfloat16), "tensor").astype(jnp.float32)
    normed_mlp = plain_rms_scale(mixed, mlp_gain)
    gate_rows = w_gate.astype(jnp.bfloat16)
    up_rows = w_up.astype(jnp.bfloat16)
    gate_sum, up_sum = contract_rows(
        normed_mlp,
        (
            lax.all_gather(gate_rows, "group", axis=0, tiled=True),
            lax.all_gather(up_rows, "group", axis=0, tiled=True),
        ),
    )
    activation = (jax.nn.silu(gate_sum) * up_sum).astype(jnp.bfloat16)
    down_rows = w_down.astype(jnp.bfloat16)
    down_part = jnp.dot(
        activation,
        lax.all_gather(down_rows, "group", axis=1, tiled=True),
        preferred_element_type=jnp.float32,
    )
    summed = lax.psum(down_part.astype(jnp.bfloat16), "tensor").astype(jnp.float32)
    first_row = lax.axis_index("tensor") * rows_dev
    own_mixed = lax.dynamic_slice_in_dim(mixed, first_row, rows_dev, 0)
    own_summed = lax.dynamic_slice_in_dim(summed, first_row, rows_dev, 0)
    layer_out = (own_mixed + own_summed).astype(jnp.bfloat16)
    pages = page_table.shape[1]
    changed = jnp.concatenate(
        [jnp.ones((1,), jnp.int32), (request_of[1:] != request_of[:-1]).astype(jnp.int32)]
    )
    opens = jnp.maximum(changed, (positions % PAGE == 0).astype(jnp.int32))
    logical = jnp.cumsum(opens) - 1
    chosen = jnp.sum(
        jnp.where(logical[:, None] == jnp.arange(pages)[None, :], page_table, 0), axis=1
    )
    target = chosen * PAGE + positions % PAGE
    width = 2 * KVH * HD // tensor_count
    flat_rows = kv_rows.reshape(tok_group, key_heads * 2 * HD)
    offset = lax.axis_index("tensor") * width % (key_heads * 2 * HD)
    own_slice = lax.dynamic_slice_in_dim(flat_rows, offset, width, 1)
    cache = jnp.zeros((pages * PAGE, width), jnp.bfloat16).at[target].set(own_slice)
    return (layer_out, cache.reshape(pages, PAGE, width))


def solution(mesh):
    shaped = mesh.shape["tensor"] == len(ORDER) and mesh.shape["group"] == 4
    placed = (
        P(("group", "tensor"), None),
        P("group"),
        P("group"),
        P("group", None),
        P(),
        P(),
        P("group", "tensor"),
        P("group", "tensor"),
        P("group", "tensor"),
        P("tensor", "group"),
        P("group", "tensor"),
        P("group", "tensor"),
        P("tensor", "group"),
    )
    return jax.shard_map(
        body if shaped else plain_body,
        mesh=mesh,
        in_specs=placed,
        out_specs=(P(("group", "tensor"), None), P("group", None, "tensor")),
        check_vma=False,
    )
```

```python
import functools

import jax
import jax.numpy as jnp
from jax import lax
from jax.experimental import pallas as pl
from jax.experimental.pallas import tpu as pltpu
from jax.sharding import PartitionSpec as P

QH = 16
KVH = 8
HD = 128
PAGE = 128
REACH = 512

rope_base = 1000000.0
norm_eps = 1e-06

F32 = jnp.float32
BF16 = jnp.bfloat16

ORDER = (2, 6, 4, 0, 3, 7, 5, 1)


def swap(value, distance):
    return lax.ppermute(
        value, "tensor", [(i, i ^ distance) for i in range(lax.axis_size("tensor"))]
    )


def turn(value, distance):
    count = lax.axis_size("group")
    return lax.ppermute(value, "group", [(i, (i + distance) % count) for i in range(count)])


def pair_swap(value):
    return lax.ppermute(value, "group", [(i, i ^ 1) for i in range(lax.axis_size("group"))])


def gather_alternate(value):
    count = lax.axis_size("group")
    return lax.all_gather(
        value,
        "group",
        axis=0,
        tiled=True,
        axis_index_groups=[list(range(m, count, 2)) for m in range(2)],
    )


def from_behind(block):
    count = lax.axis_size("group")
    return lax.ppermute(block, "group", [(i, i + 1) for i in range(count - 1)])


def tied(*values):
    return lax.optimization_barrier(values)


def step(started, function, *operands):
    shapes = jax.eval_shape(function, *operands)

    def nothing(*operands):
        return jax.tree.map(lambda leaf: jnp.zeros(leaf.shape, leaf.dtype), shapes)

    return lax.cond(started, function, nothing, *operands)


def after(value, *others):
    return lax.optimization_barrier((value, *others))[0]


def rms_scale(values, gain):
    square = jnp.mean(values * values, axis=-1, keepdims=True)
    return (values * lax.rsqrt(square + norm_eps) * gain).astype(BF16)


def gather_first(own):
    return swap(own, 2), swap(own, 4)


def gather_far(firsts):
    by_x, by_y = firsts
    half = by_x.shape[0] // 2
    return swap(by_x[:half], 4), swap(by_y[half:], 2)


def near_blocks(own, firsts, far):
    return [firsts[0], far[0], far[1], firsts[1], own]


def over(near):
    return [swap(block, 1) for block in near]


def wide_sum(*terms):
    total = terms[0].astype(F32)
    for term in terms[1:]:
        total = total + term.astype(F32)
    return total


def scatter_first(mine, other, earlier=None):
    got_left, got_right = (swap(half, 1) for half in other)
    if earlier is not None:
        got_left, got_right = after((got_left, got_right), earlier)
    left, right = mine
    rows = left.shape[0] // 4
    left_in = swap(wide_sum(left[: 2 * rows], got_left[: 2 * rows]).astype(BF16), 2)
    right_in = swap(wide_sum(right[rows : 3 * rows], got_right[rows : 3 * rows]).astype(BF16), 4)
    return left, right, got_left, got_right, left_in, right_in


def scatter_last(parts):
    left, right, got_left, got_right, left_in, right_in = parts
    rows = left.shape[0] // 4
    two, three = 2 * rows, 3 * rows
    left_on = wide_sum(left[two:three], got_left[two:three], left_in[rows:]).astype(BF16)
    right_on = wide_sum(right[:rows], got_right[:rows], right_in[:rows]).astype(BF16)
    left_last = swap(left_on, 4)
    right_last = swap(right_on, 2)
    return jnp.concatenate(
        [
            wide_sum(left[three:], got_left[three:], left_in[:rows], left_last),
            wide_sum(right[three:], got_right[three:], right_in[rows:], right_last),
        ],
        axis=1,
    )


def pack_kernel(*refs):
    out_ref = refs[-1]
    at = 0
    for ref in refs[:-1]:
        width = ref.shape[1]
        out_ref[:, at : at + width] = ref[...].astype(BF16)
        at += width


def pack(*weights):
    vmem = pl.BlockSpec(memory_space=pltpu.VMEM)
    width = sum(weight.shape[1] for weight in weights)
    return pl.pallas_call(
        pack_kernel,
        in_specs=[vmem] * len(weights),
        out_specs=vmem,
        out_shape=jax.ShapeDtypeStruct((weights[0].shape[0], width), BF16),
        name="pack",
    )(*weights)


def project_kernel(blocks, places, *refs):
    rows, (w_ref, cos_ref, sin_ref, q_ref, kv_ref) = refs[:blocks], refs[blocks:]
    heads = q_ref.shape[1] // HD
    for b, block in enumerate(rows):
        size = block.shape[0]
        raw = jnp.dot(block[...], w_ref[...], preferred_element_type=F32).astype(BF16)
        here = pl.ds(pl.multiple_of(places[b], 32), size)
        cosine = cos_ref[here, :]
        sine = sin_ref[here, :]

        def rotated(head):
            wide = raw[:, head * HD : (head + 1) * HD].astype(F32)
            turned = jnp.concatenate([wide[:, HD // 2 :], wide[:, : HD // 2]], axis=1)
            return (wide * cosine + turned * sine).astype(BF16)

        for head in range(heads):
            q_ref[here, head * HD : (head + 1) * HD] = rotated(head)
        kv_ref[here, :HD] = rotated(heads)
        kv_ref[here, HD:] = raw[:, (heads + 1) * HD :]


def project(blocks, weight, cosine, sine, places):
    rows = cosine.shape[0]
    depth, width = weight.shape
    vmem = pl.BlockSpec(memory_space=pltpu.VMEM)
    smem = pl.BlockSpec(memory_space=pltpu.SMEM)
    return pl.pallas_call(
        functools.partial(project_kernel, len(blocks)),
        in_specs=[smem] + [vmem] * (len(blocks) + 3),
        out_specs=[vmem, vmem],
        out_shape=[
            jax.ShapeDtypeStruct((rows, width - 2 * HD), BF16),
            jax.ShapeDtypeStruct((rows, 2 * HD), BF16),
        ],
        compiler_params=pltpu.CompilerParams(vmem_limit_bytes=40 * 1024 * 1024),
        cost_estimate=pl.CostEstimate(
            flops=2 * rows * depth * width,
            bytes_accessed=2 * (rows * depth + depth * width),
            transcendentals=0,
        ),
        name="project",
    )(places, *blocks, weight, cosine, sine)


def attend_kernel(q_ref, kv_ref, pos_ref, out_ref):
    step = pl.program_id(0)
    size = q_ref.shape[0]
    span = size + REACH
    window = pl.ds(pl.multiple_of(step * size, size), span)
    keys = kv_ref[window, :HD]
    values = kv_ref[window, HD:]
    row = lax.broadcasted_iota(jnp.int32, (size, span), 0)
    column = lax.broadcasted_iota(jnp.int32, (size, span), 1)
    back = row + REACH - column
    visible = (back >= 0) & (back <= pos_ref[...])
    for head in range(q_ref.shape[1] // HD):
        query = q_ref[:, head * HD : (head + 1) * HD]
        scores = lax.dot_general(
            query, keys, (((1,), (1,)), ((), ())), preferred_element_type=F32
        ) * HD ** (-0.5)
        scores = jnp.where(visible, scores, -1e30)
        peak = jnp.max(scores, axis=1, keepdims=True)
        probs = jnp.exp(scores - peak)
        total = jnp.sum(probs, axis=1, keepdims=True)
        mixed = jnp.dot(probs.astype(BF16), values, preferred_element_type=F32)
        out_ref[:, head * HD : (head + 1) * HD] = (mixed / total).astype(BF16)


def attend(queries, keys_values, positions, first, last):
    size = 256
    width = queries.shape[1]
    rows = last - first
    skip = first // size
    return pl.pallas_call(
        attend_kernel,
        grid=(rows // size,),
        in_specs=[
            pl.BlockSpec((size, width), lambda i: (i + skip, 0)),
            pl.BlockSpec(keys_values.shape, lambda i: (0, 0)),
            pl.BlockSpec((size, 1), lambda i: (i + skip, 0)),
        ],
        out_specs=pl.BlockSpec((size, width), lambda i: (i, 0)),
        out_shape=jax.ShapeDtypeStruct((rows, width), BF16),
        compiler_params=pltpu.CompilerParams(vmem_limit_bytes=32 * 1024 * 1024),
        cost_estimate=pl.CostEstimate(
            flops=4 * rows * (size + REACH) * width,
            bytes_accessed=4 * rows * width,
            transcendentals=rows * (size + REACH) * width // HD,
        ),
        name="attend",
    )(queries, keys_values, positions)


def mix_kernel(rows, places, x_ref, w_ref, left_ref, right_ref):
    depth = x_ref.shape[1]
    width = w_ref.shape[1]
    for b in range(places.shape[0]):
        block = x_ref[pl.ds(pl.multiple_of(places[b], 32), rows), :]
        for k in range(w_ref.shape[0] // depth):
            half = (left_ref, right_ref)[k // 2]
            at = k % 2 * width
            half[b * rows : (b + 1) * rows, at : at + width] = jnp.dot(
                block, w_ref[k * depth : (k + 1) * depth, :], preferred_element_type=F32
            ).astype(BF16)


def mix(attended, weight, places, rows):
    count = places.shape[0] * rows
    depth = attended.shape[1]
    width = weight.size // depth
    vmem = pl.BlockSpec(memory_space=pltpu.VMEM)
    return pl.pallas_call(
        functools.partial(mix_kernel, rows),
        in_specs=[pl.BlockSpec(memory_space=pltpu.SMEM), vmem, vmem],
        out_specs=[vmem, vmem],
        out_shape=[jax.ShapeDtypeStruct((count, width // 2), BF16)] * 2,
        compiler_params=pltpu.CompilerParams(vmem_limit_bytes=40 * 1024 * 1024),
        cost_estimate=pl.CostEstimate(
            flops=2 * count * depth * width,
            bytes_accessed=2 * count * width,
            transcendentals=0,
        ),
        name="mix",
    )(places, attended, weight)


def gate_kernel(blocks, sources, *refs):
    rows, pieces, (out_ref, held) = refs[:blocks], refs[blocks:-2], refs[-2:]
    depth = rows[0].shape[1] // sources.shape[0]
    start = 0
    for block in rows:
        stop = start + block.shape[0]
        for k in range(sources.shape[0]):
            columns = pl.ds(pl.multiple_of(sources[k] * depth, depth), depth)
            held[start:stop, k * depth : (k + 1) * depth] = block[:, columns]
        start = stop
    width = out_ref.shape[1]
    tile = width // 2
    for at in range(0, width, tile):
        gate = up = 0.0
        first = 0
        for piece in pieces:
            last = first + piece.shape[0]
            acts = held[:, first:last]
            gate += jnp.dot(acts, piece[:, at : at + tile], preferred_element_type=F32)
            up += jnp.dot(
                acts, piece[:, width + at : width + at + tile], preferred_element_type=F32
            )
            first = last
        out_ref[:, at : at + tile] = (gate / (1.0 + jnp.exp(-gate)) * up).astype(BF16)


def gate_up(blocks, pieces, sources):
    count = sum(block.shape[0] for block in blocks)
    depth = blocks[0].shape[1]
    width = pieces[0].shape[1]
    vmem = pl.BlockSpec(memory_space=pltpu.VMEM)
    return pl.pallas_call(
        functools.partial(gate_kernel, len(blocks)),
        in_specs=[pl.BlockSpec(memory_space=pltpu.SMEM)] + [vmem] * (len(blocks) + len(pieces)),
        out_specs=vmem,
        out_shape=jax.ShapeDtypeStruct((count, width // 2), BF16),
        scratch_shapes=[pltpu.VMEM((count, depth), BF16)],
        compiler_params=pltpu.CompilerParams(vmem_limit_bytes=40 * 1024 * 1024),
        cost_estimate=pl.CostEstimate(
            flops=2 * count * depth * width,
            bytes_accessed=2 * (count * depth + depth * width),
            transcendentals=count * width // 2,
        ),
        name="gate_up",
    )(sources, *blocks, *pieces)


def down_kernel(acts_ref, *refs):
    pieces, out_ref = refs[:-1], refs[-1]
    depth = acts_ref.shape[1]
    width = pieces[0].shape[1]
    slices = [(piece, at) for piece in pieces for at in range(0, piece.shape[0], depth)]
    for k, (piece, at) in enumerate(slices):
        out_ref[:, k * width : (k + 1) * width] = jnp.dot(
            acts_ref[...], piece[at : at + depth, :], preferred_element_type=F32
        ).astype(BF16)


def down(acts, pieces):
    rows, depth = acts.shape
    width = sum(piece.size for piece in pieces) // depth
    vmem = pl.BlockSpec(memory_space=pltpu.VMEM)
    return pl.pallas_call(
        down_kernel,
        in_specs=[vmem] * (1 + len(pieces)),
        out_specs=vmem,
        out_shape=jax.ShapeDtypeStruct((rows, width), BF16),
        compiler_params=pltpu.CompilerParams(vmem_limit_bytes=40 * 1024 * 1024),
        cost_estimate=pl.CostEstimate(
            flops=2 * rows * depth * width,
            bytes_accessed=2 * (rows + depth) * width,
            transcendentals=0,
        ),
        name="down",
    )(acts, *pieces)


def finish_kernel(sources, pair_sources, mixed_ref, own_ref, pair_ref, out_ref, total):
    count = sources.shape[0]
    width = mixed_ref.shape[1] // count

    def at(place):
        return pl.ds(pl.multiple_of(place * width, width), width)

    for k in range(count):
        columns = at(sources[k])
        total[:, columns] = mixed_ref[:, columns] + own_ref[:, k * width : (k + 1) * width]
    for k in range(count):
        columns = at(pair_sources[k])
        pair = pair_ref[:, k * width : (k + 1) * width].astype(F32)
        out_ref[:, columns] = (total[:, columns] + pair).astype(BF16)


def finish(mixed, own, pair, sources, pair_sources):
    vmem = pl.BlockSpec(memory_space=pltpu.VMEM)
    smem = pl.BlockSpec(memory_space=pltpu.SMEM)
    return pl.pallas_call(
        finish_kernel,
        in_specs=[smem, smem, vmem, vmem, vmem],
        out_specs=vmem,
        out_shape=jax.ShapeDtypeStruct(mixed.shape, BF16),
        scratch_shapes=[pltpu.VMEM(mixed.shape, F32)],
        compiler_params=pltpu.CompilerParams(vmem_limit_bytes=16 * 1024 * 1024),
        name="finish",
    )(sources, pair_sources, mixed, own, pair)


def body(
    hidden,
    request_of,
    positions,
    page_table,
    attn_gain,
    mlp_gain,
    wq,
    wk,
    wv,
    wo,
    w_gate,
    w_up,
    w_down,
):
    groups = lax.axis_size("group")
    me = lax.axis_index("tensor")
    group = lax.axis_index("group")
    odd = group % 2 == 1
    tok_group = request_of.shape[0]
    depth = hidden.shape[1]
    rows_dev = hidden.shape[0]
    def order_of(plane):
        alike = [plane % 2 + k for k in range(0, groups, 2)]
        return jnp.stack(alike + [(plane - k) % groups for k in (1, 3)]).astype(jnp.int32)

    sources, pair_sources = order_of(group), order_of(group ^ 1)
    starts = []
    for k in ORDER:
        first = (me ^ k) * rows_dev
        starts += [first, first + rows_dev // 2] if k in (6, 7) else [first]
    places = jnp.stack(starts).astype(jnp.int32)

    small = pack(wq, wk, wv)
    qkv_weight = lax.all_gather(small, "group", axis=0, tiled=True)
    own_normed = rms_scale(hidden.astype(F32), attn_gain)
    firsts = gather_first(own_normed)
    ff = w_gate.shape[1] // 2
    gate_b, up_b, down_b = w_gate.astype(BF16), w_up.astype(BF16), w_down.astype(BF16)
    lower = jnp.concatenate([gate_b[:, :ff], up_b[:, :ff]], axis=1)
    upper = jnp.concatenate([gate_b[:, ff:], up_b[:, ff:]], axis=1)
    mine_in = jnp.where(odd, upper, lower)
    other_in = jnp.where(odd, lower, upper)
    mine_out = jnp.where(odd, down_b[ff:], down_b[:ff])
    other_out = jnp.where(odd, down_b[:ff], down_b[ff:])
    firsts, mine_in, other_in, mine_out, other_out = tied(
        firsts, mine_in, other_in, mine_out, other_out
    )
    far = gather_far(firsts)
    near = near_blocks(own_normed, firsts, far)
    normed = near + over(near)
    out_weight = lax.all_gather(wo.astype(BF16), "group", axis=0, tiled=True)

    half_dim = HD // 2
    frequency = rope_base ** (-(jnp.arange(half_dim, dtype=F32) * 2.0 / HD))
    angle = positions.astype(F32)[:, None] * frequency[None, :]
    cosine, sine = jnp.cos(angle), jnp.sin(angle)
    cosine = jnp.concatenate([cosine, cosine], axis=1)
    sine = jnp.concatenate([-sine, sine], axis=1)

    queries, kv_rows = project(normed, qkv_weight, cosine, sine, places)
    earlier = from_behind(kv_rows[-REACH:])
    places_in = positions[:, None]
    late = attend(queries, kv_rows, places_in, REACH, tok_group)
    early_kv = jnp.concatenate([earlier, kv_rows[:REACH]], axis=0)
    early = attend(queries, early_kv, places_in, 0, REACH)
    attended = jnp.concatenate([early, late], axis=0)

    started = positions[0] >= 0

    alike_in = gather_alternate(after(mine_in, kv_rows))
    alike_out = gather_alternate(after(mine_out, kv_rows))

    pages = page_table.shape[1]
    changed = jnp.concatenate(
        [jnp.ones((1,), jnp.int32), (request_of[1:] != request_of[:-1]).astype(jnp.int32)]
    )
    opens = jnp.maximum(changed, (positions % PAGE == 0).astype(jnp.int32))
    logical = jnp.cumsum(opens) - 1
    chosen = jnp.sum(
        jnp.where(logical[:, None] == jnp.arange(pages)[None, :], page_table, 0), axis=1
    )
    target = chosen * PAGE + positions % PAGE
    width = kv_rows.shape[1]

    four = len(ORDER) // 2
    block_places = jnp.stack([(me ^ k) * rows_dev for k in ORDER]).astype(jnp.int32)

    def to_blocks(attended, out_weight, block_places, hidden, gain, other_in, target, kv_rows):
        other = mix(attended, out_weight, block_places[four:], rows_dev)
        mine = mix(attended, out_weight, block_places[:four], rows_dev)
        mixed = hidden.astype(F32) + scatter_last(scatter_first(mine, other))
        own_rows = rms_scale(mixed, gain)
        pair_rows = pair_swap(own_rows)
        firsts = gather_first(own_rows)
        cache = jnp.zeros((pages * PAGE, kv_rows.shape[1]), BF16).at[target].set(kv_rows)
        firsts, cache = tied(firsts, cache)
        own_near = near_blocks(own_rows, firsts, gather_far(firsts))
        own_blocks = [own_near, over(own_near)]
        near_in = turn(after(other_in, own_near), 1)
        firsts = gather_first(after(pair_rows, own_near))
        firsts, near_in = tied(firsts, near_in)
        far_in = turn(after(other_in, pair_rows), 3)
        pair_near = near_blocks(pair_rows, firsts, gather_far(firsts))
        return mixed, own_blocks, [pair_near, over(pair_near)], near_in, far_in, cache

    mixed, own_blocks, other_blocks, near_in, far_in, cache = step(
        started,
        to_blocks,
        attended,
        out_weight,
        block_places,
        hidden,
        mlp_gain,
        other_in,
        target,
        kv_rows,
    )
    in_pieces = [alike_in, near_in, far_in]
    own_blocks, alike_out = tied(own_blocks, alike_out)
    other_out = after(other_out, far_in)
    near_out, far_out = turn(other_out, 1), turn(other_out, 3)

    def acts_of(blocks):
        near, across = blocks
        return gate_up(across, in_pieces, sources), gate_up(near, in_pieces, sources)

    own_acts = acts_of(own_blocks)
    other_acts = acts_of(other_blocks)
    left = [down(half, [alike_out]) for half in other_acts]
    other_acts, own_across, out_pieces = tied(other_acts, own_acts[0], [near_out, far_out])
    own_acts = (own_across, own_acts[1])
    right = [down(half, out_pieces) for half in other_acts]
    pair_parts = scatter_first((left[1], right[1]), (left[0], right[0]))
    own_acts = after(own_acts, pair_parts[:4])
    left = [down(half, [alike_out]) for half in own_acts]
    right = [down(half, out_pieces) for half in own_acts]
    mine, other = (left[1], right[1]), (left[0], right[0])
    own_parts = scatter_first(mine, other, pair_parts)
    pair_sum = scatter_last(pair_parts).astype(BF16)
    from_pair = pair_swap(pair_sum)
    own_parts = after(own_parts, from_pair)
    own_sum = scatter_last(own_parts)
    layer_out = finish(mixed, own_sum, from_pair, sources, pair_sources)
    return (layer_out, cache.reshape(pages, PAGE, width))


def partner(value, axis, distance):
    mask = 2**distance
    pairs = [(source, source ^ mask) for source in range(lax.axis_size(axis))]
    return lax.ppermute(value, axis, pairs)


def plain_from_behind(block, axis, distance):
    devices = range(lax.axis_size(axis))
    route = [(i - distance, i) for i in devices if i - distance in devices]
    return lax.ppermute(block, axis, route)


def plain_rms_scale(values, gain):
    square = jnp.mean(values * values, axis=-1, keepdims=True)
    return (values * lax.rsqrt(square + norm_eps) * gain).astype(jnp.bfloat16)


def rotate(values, places):
    half_dim = values.shape[-1] // 2
    frequency = rope_base ** (-(jnp.arange(half_dim, dtype=jnp.float32) * 2.0 / values.shape[-1]))
    angle = places.astype(jnp.float32)[:, None] * frequency[None, :]
    cosine = jnp.cos(angle)[:, None, :]
    sine = jnp.sin(angle)[:, None, :]
    widened = values.astype(jnp.float32)
    first = widened[..., :half_dim]
    second = widened[..., half_dim:]
    return jnp.concatenate(
        [first * cosine - second * sine, second * cosine + first * sine], axis=-1
    ).astype(jnp.bfloat16)


def join_halves(own_part, other_part):
    even = lax.axis_index("tensor") % 2 == 0
    lower = jnp.where(even, own_part, other_part)
    upper = jnp.where(even, other_part, own_part)
    return jnp.concatenate([lower, upper], axis=-1)


def contract_rows(acts, pieces):
    return tuple((jnp.dot(acts, piece, preferred_element_type=jnp.float32) for piece in pieces))


def plain_body(
    hidden,
    request_of,
    positions,
    page_table,
    attn_gain,
    mlp_gain,
    wq,
    wk,
    wv,
    wo,
    w_gate,
    w_up,
    w_down,
):
    tensor_count = lax.axis_size("tensor")
    rows_dev = hidden.shape[0]
    tok_group = request_of.shape[0]
    query_heads = QH // tensor_count
    key_heads = max(1, KVH // tensor_count)
    group_ratio = QH // KVH
    paired = tensor_count > KVH
    residual = lax.all_gather(hidden, "tensor", axis=0, tiled=True).astype(jnp.float32)
    normed = plain_rms_scale(residual, attn_gain)
    query_rows = wq.astype(jnp.bfloat16)
    key_rows = wk.astype(jnp.bfloat16)
    value_rows = wv.astype(jnp.bfloat16)
    if paired:
        other_key, other_value = partner((key_rows, value_rows), "tensor", 0)
        key_rows = join_halves(key_rows, other_key)
        value_rows = join_halves(value_rows, other_value)
    query_sum, key_sum, value_sum = contract_rows(
        normed,
        (
            lax.all_gather(query_rows, "group", axis=0, tiled=True),
            lax.all_gather(key_rows, "group", axis=0, tiled=True),
            lax.all_gather(value_rows, "group", axis=0, tiled=True),
        ),
    )
    query_raw = query_sum.astype(jnp.bfloat16)
    key_raw = key_sum.astype(jnp.bfloat16)
    value_raw = value_sum.astype(jnp.bfloat16)
    queries = rotate(query_raw.reshape(tok_group, query_heads, HD), positions)
    keys = rotate(key_raw.reshape(tok_group, key_heads, HD), positions)
    values = value_raw.reshape(tok_group, key_heads, HD)
    kv_rows = jnp.stack([keys, values], axis=2)
    earlier = plain_from_behind(kv_rows, "group", 1)
    earlier_rows = earlier.shape[0]
    all_rows = jnp.concatenate([earlier, kv_rows], axis=0)
    all_keys = jnp.repeat(all_rows[:, :, 0], group_ratio, axis=1)[:, :query_heads]
    all_values = jnp.repeat(all_rows[:, :, 1], group_ratio, axis=1)[:, :query_heads]
    first_request = request_of[0]
    first_position = positions[0]
    same_local = (request_of[:, None] == request_of[None, :]) & (
        positions[None, :] <= positions[:, None]
    )
    same_earlier = (request_of[:, None] == first_request) & (
        jnp.arange(earlier_rows)[None, :] >= earlier_rows - first_position
    )
    visible = jnp.concatenate([same_earlier, same_local], axis=1)
    scores = jnp.einsum(
        "qhd,khd->hqk", queries, all_keys, preferred_element_type=jnp.float32
    ) * HD ** (-0.5)
    scores = jnp.where(visible[None], scores, -1e30)
    row_peak = jnp.max(scores, axis=-1, keepdims=True)
    probs = jnp.where(visible[None], jnp.exp(scores - row_peak), 0.0)
    total = jnp.sum(probs, axis=-1, keepdims=True)
    mixed_heads = jnp.einsum(
        "hqk,khd->qhd", probs.astype(jnp.bfloat16), all_values, preferred_element_type=jnp.float32
    ) / jnp.transpose(total, (1, 0, 2))
    attended = mixed_heads.astype(jnp.bfloat16).reshape(tok_group, query_heads * HD)
    out_rows = wo.astype(jnp.bfloat16)
    attn_part = jnp.dot(
        attended,
        lax.all_gather(out_rows, "group", axis=1, tiled=True),
        preferred_element_type=jnp.float32,
    )
    mixed = residual + lax.psum(attn_part.astype(jnp.bfloat16), "tensor").astype(jnp.float32)
    normed_mlp = plain_rms_scale(mixed, mlp_gain)
    gate_rows = w_gate.astype(jnp.bfloat16)
    up_rows = w_up.astype(jnp.bfloat16)
    gate_sum, up_sum = contract_rows(
        normed_mlp,
        (
            lax.all_gather(gate_rows, "group", axis=0, tiled=True),
            lax.all_gather(up_rows, "group", axis=0, tiled=True),
        ),
    )
    activation = (jax.nn.silu(gate_sum) * up_sum).astype(jnp.bfloat16)
    down_rows = w_down.astype(jnp.bfloat16)
    down_part = jnp.dot(
        activation,
        lax.all_gather(down_rows, "group", axis=1, tiled=True),
        preferred_element_type=jnp.float32,
    )
    summed = lax.psum(down_part.astype(jnp.bfloat16), "tensor").astype(jnp.float32)
    first_row = lax.axis_index("tensor") * rows_dev
    own_mixed = lax.dynamic_slice_in_dim(mixed, first_row, rows_dev, 0)
    own_summed = lax.dynamic_slice_in_dim(summed, first_row, rows_dev, 0)
    layer_out = (own_mixed + own_summed).astype(jnp.bfloat16)
    pages = page_table.shape[1]
    changed = jnp.concatenate(
        [jnp.ones((1,), jnp.int32), (request_of[1:] != request_of[:-1]).astype(jnp.int32)]
    )
    opens = jnp.maximum(changed, (positions % PAGE == 0).astype(jnp.int32))
    logical = jnp.cumsum(opens) - 1
    chosen = jnp.sum(
        jnp.where(logical[:, None] == jnp.arange(pages)[None, :], page_table, 0), axis=1
    )
    target = chosen * PAGE + positions % PAGE
    width = 2 * KVH * HD // tensor_count
    flat_rows = kv_rows.reshape(tok_group, key_heads * 2 * HD)
    offset = lax.axis_index("tensor") * width % (key_heads * 2 * HD)
    own_slice = lax.dynamic_slice_in_dim(flat_rows, offset, width, 1)
    cache = jnp.zeros((pages * PAGE, width), jnp.bfloat16).at[target].set(own_slice)
    return (layer_out, cache.reshape(pages, PAGE, width))


def solution(mesh):
    shaped = mesh.shape["tensor"] == len(ORDER) and mesh.shape["group"] == 4
    placed = (
        P(("group", "tensor"), None),
        P("group"),
        P("group"),
        P("group", None),
        P(),
        P(),
        P("group", "tensor"),
        P("group", "tensor"),
        P("group", "tensor"),
        P("tensor", "group"),
        P("group", "tensor"),
        P("group", "tensor"),
        P("tensor", "group"),
    )
    return jax.shard_map(
        body if shaped else plain_body,
        mesh=mesh,
        in_specs=placed,
        out_specs=(P(("group", "tensor"), None), P("group", None, "tensor")),
        check_vma=False,
    )
```
